1024 devices in a mesh: dp: 16 (over x, y), expert: 64 (over z, core).
Axes of the slice: x: 4, y: 4, z: 32, core: 2. Of those that a mesh axis runs over, the one named last changes fastest.
Arguments:
- tokens: bfloat16 [2048, 64, 1024], P(('dp', 'expert')), may hold values from -8 to 8
- expert_ids: int32 [2048, 64, 1], P(('dp', 'expert')), may hold values from 0 to 31; in each aligned block of 128 rows (0 to 127, 128 to 255, ..., all dimensions but the last counted through in order) at most 6 rows name the same one
- caption_len: int32 [2048], P(('dp', 'expert')), may hold values from 1 to 16, as said below
- router: bfloat16 [1024, 32], replicated, may hold values from -0.1875 to 0.1875
- expert_in: bfloat16 [64, 1024, 2048], P('expert'), may hold values from -0.1875 to 0.1875
- expert_out: bfloat16 [64, 2048, 1024], P('expert'), may hold values from -0.09375 to 0.09375
Outputs:
- layer_out: bfloat16 [2048, 64, 1024], P(('dp', 'expert'))
- pair_loss: float32 [2048], P(('dp', 'expert'))
The draws below stay inside these ranges and needn't reach their ends.
Inputs may be any that keep to these rules, and one draw needn't show every extreme that they name: `expert_ids`: in the 128 tokens of one device no expert is named more than 6 times, a bound that some block reaches. `caption_len`: the first pair of every device has a caption of full length.
All inputs are finite; a program needn't handle non-finite values.
Results may differ from the reference program's by a relative error of at most 0.008.
Values may be sent and summed in bfloat16 or wider, within the bound.
A program may use at most 64 MiB of HBM per device.

```python
import math
import jax
import jax.numpy as jnp
import numpy as np
from jax import lax

D = 1024
FF = 4096
PAIRS_DEV = 2
IMG_TOK = 48
TXT_TOK = 16
SEQ = 64
TOK_DEV = 128
EXPERTS = 32
CAP = 6
PAIRS = 2048
N_DP = 16
N_EXPERT = 64


def draw_tokens(key, part):
    key = jax.random.fold_in(key, 11)
    base_key, shared_key, center_key, order_key = jax.random.split(key, 4)
    base = jax.random.normal(base_key, (PAIRS, SEQ, D), jnp.float32)
    shared = jax.random.normal(shared_key, (PAIRS, D), jnp.float32)
    groups = max(PAIRS // 16, 1)
    centers = jax.random.normal(center_key, (groups, D), jnp.float32)
    member = jax.random.permutation(order_key, PAIRS) % groups
    cluster = centers[member]
    image_part = 0.1 * shared[:, None, :] + 0.15 * cluster[:, None, :]
    text_part = 0.15 * shared[:, None, :] + 0.2 * cluster[:, None, :]
    is_image = (jnp.arange(SEQ) < IMG_TOK)[None, :, None]
    signal = jnp.where(is_image, image_part, text_part)
    return jnp.clip(base + signal, -8.0, 8.0).astype(jnp.bfloat16)


def draw_caption_len(key, part):
    key = jax.random.fold_in(key, 23)
    lengths = jax.random.randint(key, (PAIRS,), 1, TXT_TOK + 1)
    leading = jnp.arange(PAIRS) % PAIRS_DEV == 0
    return jnp.where(leading, TXT_TOK, lengths).astype(jnp.int32)


def block_levels(own_key, extent, pieces, least, largest):
    loudness = 1.0
    for dim, parts in pieces:
        draws = jax.random.uniform(jax.random.fold_in(jax.random.fold_in(own_key, 6), dim), (parts,), jnp.float32, least / len(pieces), largest / len(pieces))
        loudness = loudness * jnp.repeat(jnp.exp(draws), extent[dim] // parts).reshape((-1,) + (1,) * (len(extent) - 1 - dim))
    return loudness


def shared_out(own_key, own, number, rows, number_of, top, limit, lean):
    ranking = jax.random.permutation(own_key, number_of)
    packed, ordinary = portions_of(number_of, rows * top, limit, lean, True), portions_of(number_of, rows * top, limit, lean, False)
    places = jnp.arange(number_of)

    def named(sizes, turn):
        used = int((sizes > 0).sum())
        fixed = max(1, used // 4)
        shifted = fixed + (places - fixed + turn * (used - fixed)) % max(1, number_of - fixed)
        return jnp.zeros((number_of,), jnp.int32).at[ranking[jnp.where(places < fixed, places, shifted)]].set(jnp.asarray(sizes, jnp.int32))

    sizes = jnp.where(number % 4 == 0, named(packed, number // 4), named(ordinary, number - number // 4 - 1))
    mixed = jax.random.permutation(jax.random.fold_in(own, 3), number_of)
    giver, sink = mixed[0:number_of // 2 * 2:2], mixed[1:number_of // 2 * 2:2]
    margin = jnp.minimum(sizes[giver] - 1, limit - sizes[sink]) // 2
    margin = jnp.where((giver == ranking[0]) | (sink == ranking[0]) | (sizes[sink] == 0), 0, jnp.maximum(margin, 0))
    shifted = jax.random.randint(jax.random.fold_in(own, 4), (number_of // 2,), 0, 1 << 20) % (margin + 1)
    sizes = sizes.at[giver].add(-shifted).at[sink].add(shifted)
    items = jnp.searchsorted(jnp.cumsum(sizes), jnp.arange(rows * top), side="right").astype(jnp.int32)
    grid = items.reshape(top, rows).T
    grid = grid[jax.random.permutation(jax.random.fold_in(own, 1), rows)]
    turn = jax.random.randint(jax.random.fold_in(own, 2), (rows, 1), 0, top)
    return jnp.take_along_axis(grid, (jnp.arange(top)[None, :] + turn) % top, axis=1)


def portions_of(number_of, total, bound, skew, full):
    portions = [(1 << 20) // math.isqrt(grade ** skew) + 1 for grade in range(1, number_of + 1)]
    largest = bound if full else min(bound, max(-(-total // number_of), total * portions[0] // sum(portions)))
    least = 1 if total - largest >= number_of - 1 else 0
    counts, surplus = [largest] + [least] * (number_of - 1), total - largest - least * (number_of - 1)
    while surplus > 0:
        movable = [i for i in range(1, number_of) if counts[i] < largest] or [i for i in range(1, number_of) if counts[i] < bound]
        pool, left = sum([portions[i] for i in movable]), surplus
        for i in movable:
            addition = min(bound - counts[i], max(1, left * portions[i] // pool), surplus)
            counts[i] = counts[i] + addition
            surplus = surplus - addition
    return np.array(counts)


def bell_draw(key, shape, width, bound, shards=(), kind=jnp.bfloat16):
    result = width * jax.random.normal(key, shape, jnp.float32)
    if shards:
        result = result * block_levels(key, shape, shards, -0.22, 0.18)
    return jnp.clip(result, -bound, bound).astype(kind)


def setup_inputs(seed: int = 0) -> dict:
    streams_of = jax.random.split(jax.random.key(seed), 7)
    tokens = draw_tokens(jax.random.fold_in(streams_of[6], 71), 0)
    expert_ids_keys = jax.random.split(jax.random.fold_in(streams_of[1], 1), PAIRS * SEQ // TOK_DEV)
    expert_ids_turns = jax.random.permutation(jax.random.fold_in(streams_of[1], 3), PAIRS * SEQ // TOK_DEV)
    expert_ids = jax.vmap(lambda own, number: shared_out(jax.random.fold_in(streams_of[1], 2), own, number, TOK_DEV, EXPERTS, 1, CAP, 2))(expert_ids_keys, expert_ids_turns).reshape((PAIRS, SEQ, 1))
    caption_len = draw_caption_len(jax.random.fold_in(streams_of[6], 71), 0)
    router = bell_draw(streams_of[3], (D, EXPERTS), D ** -0.5, 0.1875)
    expert_in = bell_draw(streams_of[4], (2 * EXPERTS, D, FF // 2), D ** -0.5, 0.1875, ((0, 64),))
    expert_out = bell_draw(streams_of[5], (2 * EXPERTS, FF // 2, D), FF ** -0.5, 0.09375, ((0, 64),))
    return dict(tokens=tokens, expert_ids=expert_ids, caption_len=caption_len, router=router, expert_in=expert_in, expert_out=expert_out)


logit_scale = 20.0
norm_eps = 1e-06

def apply_expert(operands):
    grouped_rows, first_layer, second_layer = operands
    partials = []
    for which_half in range(2):
        hidden = jax.nn.gelu(jnp.dot(grouped_rows, first_layer[which_half], preferred_element_type=jnp.float32)).astype(jnp.bfloat16)
        partials.append(jnp.dot(hidden, second_layer[which_half], preferred_element_type=jnp.float32).astype(jnp.bfloat16))
    return (partials[0].astype(jnp.float32) + partials[1].astype(jnp.float32)).astype(jnp.bfloat16)

def unit_rows(vectors):
    squared_total = lax.optimization_barrier(jnp.sum(vectors * vectors, axis=-1, keepdims=True)) + norm_eps
    return (vectors * lax.rsqrt(squared_total)).astype(jnp.bfloat16)

def reference(tokens, expert_ids, caption_len, router, expert_in, expert_out):
    devices = N_DP * N_EXPERT
    row_count = PAIRS_DEV * SEQ
    token_rows = tokens.reshape(devices, row_count, D)
    chosen_ids = expert_ids.reshape(devices, row_count).astype(jnp.int32)
    onehot = chosen_ids[:, :, None] == jnp.arange(EXPERTS, dtype=jnp.int32)[None, None, :]
    running = jnp.cumsum(onehot.astype(jnp.int32), axis=1) - 1
    position = lax.optimization_barrier(jnp.sum(jnp.where(onehot, running, 0), axis=2)).astype(jnp.int32)
    slot_index = (chosen_ids * CAP + position).astype(jnp.int32)
    device_index = jnp.broadcast_to(jnp.arange(devices, dtype=jnp.int32)[:, None], (devices, row_count))
    buffer = jnp.zeros((devices, EXPERTS * CAP, D), jnp.bfloat16).at[device_index, slot_index].set(token_rows)
    grouped = buffer.reshape(devices, EXPERTS, CAP, D).transpose(1, 0, 2, 3).reshape(EXPERTS, devices * CAP, D)
    first_pairs = expert_in.reshape(EXPERTS, 2, D, FF // 2)
    second_pairs = expert_out.reshape(EXPERTS, 2, FF // 2, D)
    values = lax.map(apply_expert, (grouped, first_pairs, second_pairs))
    slot_values = values.reshape(EXPERTS, devices, CAP, D).transpose(1, 0, 2, 3).reshape(devices, EXPERTS * CAP, D)
    token_values = slot_values[device_index, slot_index].astype(jnp.float32)
    logits = jnp.dot(tokens.reshape(devices * row_count, D), router, preferred_element_type=jnp.float32).reshape(devices, row_count, EXPERTS)
    gate_value = jax.nn.sigmoid(lax.optimization_barrier(jnp.sum(jnp.where(onehot, logits, 0.0), axis=2)))
    layer_out = (token_rows.astype(jnp.float32) + gate_value[:, :, None] * token_values).astype(jnp.bfloat16)
    layer_out = layer_out.reshape(PAIRS, SEQ, D)
    pooled_source = layer_out.astype(jnp.float32)
    image_vec = lax.optimization_barrier(jnp.mean(pooled_source[:, :IMG_TOK, :], axis=1))
    text_mask = (jnp.arange(TXT_TOK, dtype=jnp.int32)[None, :] < caption_len[:, None]).astype(jnp.float32)
    text_vec = lax.optimization_barrier(jnp.sum(pooled_source[:, IMG_TOK:, :] * text_mask[:, :, None], axis=1)) / caption_len[:, None].astype(jnp.float32)
    image_unit = unit_rows(image_vec)
    text_unit = unit_rows(text_vec)
    scores = logit_scale * jnp.dot(image_unit, text_unit.T, preferred_element_type=jnp.float32)
    weights = jnp.exp(scores)
    row_total = lax.optimization_barrier(jnp.sum(weights, axis=1))
    col_total = lax.optimization_barrier(jnp.sum(weights, axis=0))
    matched = logit_scale * lax.optimization_barrier(jnp.sum(image_unit.astype(jnp.float32) * text_unit.astype(jnp.float32), axis=1))
    pair_loss = 0.5 * (jnp.log(row_total) - matched) + 0.5 * (jnp.log(col_total) - matched)
    return (layer_out, pair_loss)
```

```python
import functools

import jax
import jax.numpy as jnp
from jax import lax
from jax.experimental import pallas as pl
from jax.experimental.pallas import tpu as pltpu
from jax.sharding import PartitionSpec as P

IMG_TOK = 48
LANES = 128
CORES = 2
logit_scale = 20.0
norm_eps = 1e-06
MESH = pl.DeviceIdType.MESH
bf16 = jnp.bfloat16
f32 = jnp.float32


def iota(shape, axis):
    return lax.broadcasted_iota(jnp.int32, shape, axis)


def dot(a, b):
    return jnp.dot(a, b, preferred_element_type=f32)


def dot_nt(a, b):
    return lax.dot_general(a, b, (((1,), (1,)), ((), ())), preferred_element_type=f32)


def chunk_major(blocks, chunks, rows):
    size = blocks * chunks * rows
    to = iota((size, 1), 0)
    chunk, rest = to // (blocks * rows), to % (blocks * rows)
    source = (rest // rows) * (chunks * rows) + chunk * rows + rest % rows
    return (iota((size, size), 1) == source).astype(bf16)


def block_major(blocks, chunks, rows):
    size = blocks * chunks * rows
    to = iota((size, 1), 0)
    block, rest = to // (chunks * rows), to % (chunks * rows)
    source = (rest // rows) * (blocks * rows) + block * rows + rest % rows
    return (iota((size, size), 1) == source).astype(bf16)


def kernel(
    cfg, tok, ids, clen, router_t, win_hbm, wout_hbm, out_ref, loss_ref,
    win, wout, unfold, fold, unfold_z, unfold_p, slot_col_ref, gate_ref,
    out_blocks, arrived, sib_arrived, x_rows, total,
    own_part, send_part, sib_part, ret_blocks, ret_arrived, token_total,
    units, image_blocks, text_blocks, image_rows, text_rows,
    row_vec, col_vec, row_parts, col_parts,
    w_sem, d_send, d_recv, f_send, f_recv, p_send, p_recv, r_send, r_recv,
    g_send, g_recv, s_send, s_recv,
):
    Z, DP, CAP, CH, GS, FFC = cfg
    PLANE = DP * CORES
    GROUPS = Z // GS
    BLK = CAP * CH
    ROWS = GS * CAP
    tokens = tok.shape[0]
    half = tokens // 2
    dp = lax.axis_index("dp")
    ex = lax.axis_index("expert")
    z = ex // CORES
    core = ex % CORES

    def ring(k):
        return {"dp": dp, "expert": lax.rem(z + k, Z) * CORES + core}

    def in_plane(m):
        return {
            "dp": lax.rem(dp + m // CORES, DP),
            "expert": z * CORES + lax.rem(core + m % CORES, CORES),
        }

    sibling = {"dp": dp, "expert": z * CORES + (1 - core)}

    def offset(q):
        return jnp.where(q % 2 == 1, Z // 2 - (q + 1) // 2, lax.rem(q // 2 + Z // 2, Z))

    barrier = pltpu.get_barrier_semaphore()

    def greet_ring(k, c):
        pl.semaphore_signal(barrier, inc=1, device_id=ring(k), device_id_type=MESH)
        return c

    def greet_plane(m, c):
        pl.semaphore_signal(barrier, inc=1, device_id=in_plane(m), device_id_type=MESH)
        return c

    lax.fori_loop(1, Z, greet_ring, 0)
    lax.fori_loop(1, PLANE, greet_plane, 0)

    load_in = pltpu.make_async_copy(win_hbm.at[0], win, w_sem.at[0])
    load_out = pltpu.make_async_copy(wout_hbm.at[0], wout, w_sem.at[1])
    load_in.start()
    load_out.start()

    unfold[...] = chunk_major(GS, CH, CAP)
    fold[...] = block_major(GS, CH, CAP)
    ids_row = jnp.concatenate([ids[0], ids[1]], axis=1)
    eye = iota((tokens, tokens), 0) == iota((tokens, tokens), 1)
    onehot_t = iota((Z, tokens), 0) == ids_row
    upto = (iota((tokens, tokens), 0) <= iota((tokens, tokens), 1)).astype(bf16)
    running = dot(onehot_t.astype(bf16), upto)
    position = jnp.sum(jnp.where(onehot_t, running, 0.0), axis=0, keepdims=True).astype(jnp.int32) - 1
    ahead = ids_row - z
    ahead = jnp.where(ahead < 0, ahead + Z, ahead)
    signed = jnp.where(ahead > Z // 2, ahead - Z, ahead)
    away = jnp.abs(signed)
    order = 2 * (Z // 2 - away) - jnp.where((signed >= 0) & (away < Z // 2), 1, 0)
    slot_row = order * CAP + position
    slot_col_ref[...] = jnp.sum(jnp.where(eye, slot_row.astype(f32), 0.0), axis=1, keepdims=True).astype(jnp.int32)
    ids_col = jnp.sum(jnp.where(eye, ids_row.astype(f32), 0.0), axis=1, keepdims=True).astype(jnp.int32)

    def pack(g, c):
        mask = (slot_row == g * ROWS + iota((ROWS, tokens), 0)).astype(bf16)
        rows = dot(mask, tok[...]).astype(bf16)
        stacked = jnp.concatenate([rows[:, j * LANES:(j + 1) * LANES] for j in range(CH)], axis=0)
        out_blocks[pl.ds(g * GS, GS)] = dot(fold[...], stacked).astype(bf16).reshape(GS, BLK, LANES)
        return c

    lax.fori_loop(0, GROUPS, pack, 0)

    pl.semaphore_wait(barrier, Z - 1 + PLANE - 1)

    def send_out(q, c):
        pltpu.make_async_remote_copy(
            src_ref=out_blocks.at[q], dst_ref=arrived.at[q], send_sem=d_send,
            recv_sem=d_recv.at[q // GS], device_id=ring(offset(q)), device_id_type=MESH,
        ).start()
        return c

    lax.fori_loop(0, Z - 1, send_out, 0)
    pltpu.make_async_copy(out_blocks.at[Z - 1], arrived.at[Z - 1], d_recv.at[GROUPS - 1]).start()

    logits = dot_nt(tok[...], router_t[...])
    onehot = iota((tokens, Z), 1) == ids_col
    gate_ref[...] = jax.nn.sigmoid(jnp.sum(jnp.where(onehot, logits, 0.0), axis=1, keepdims=True))
    token_total[...] = jnp.zeros_like(token_total)
    unfold_z[...] = chunk_major(Z, CH, 2)
    unfold_p[...] = chunk_major(PLANE, CH, 2)
    load_in.wait()
    load_out.wait()

    def group(ref, g):
        return ref.at[pl.ds(g * GS, GS)]

    def unpack(ref, g, base):
        blocks = ref[pl.ds(g * GS, GS)].reshape(GS * BLK, LANES)
        rows = dot(unfold[...], blocks).astype(bf16)
        for j in range(CH):
            x_rows[base:base + ROWS, j * LANES:(j + 1) * LANES] = rows[j * ROWS:(j + 1) * ROWS]

    def forward(g):
        return pltpu.make_async_remote_copy(
            src_ref=group(arrived, g), dst_ref=group(sib_arrived, g), send_sem=f_send.at[g],
            recv_sem=f_recv.at[g], device_id=sibling, device_id_type=MESH,
        )

    def swap(g):
        return pltpu.make_async_remote_copy(
            src_ref=send_part.at[g], dst_ref=sib_part.at[g], send_sem=p_send.at[g],
            recv_sem=p_recv.at[g], device_id=sibling, device_id_type=MESH,
        )

    def finish(g):
        swap(g).wait_recv()
        both = (own_part[g].astype(f32) + sib_part[g].astype(f32)).astype(bf16)
        stacked = jnp.concatenate([both[:, j * LANES:(j + 1) * LANES] for j in range(CH)], axis=0)
        ret_blocks[pl.ds(g * GS, GS)] = dot(fold[...], stacked).astype(bf16).reshape(GS, BLK, LANES)

        def send_back(i, c):
            q = g * GS + i
            pltpu.make_async_remote_copy(
                src_ref=ret_blocks.at[q], dst_ref=ret_arrived.at[q], send_sem=r_send,
                recv_sem=r_recv.at[g], device_id=ring(Z - offset(q)), device_id_type=MESH,
            ).start()
            return c

        lax.fori_loop(0, jnp.where(g == GROUPS - 1, GS - 1, GS), send_back, 0)

        @pl.when(g == GROUPS - 1)
        def _():
            pltpu.make_async_copy(ret_blocks.at[Z - 1], ret_arrived.at[Z - 1], r_recv.at[g]).start()

    def work(g, c):
        pltpu.make_async_copy(group(arrived, g), group(arrived, g), d_recv.at[g]).wait()
        forward(g).start()
        unpack(arrived, g, 0)

        @pl.when(g > 0)
        def _():
            finish(g - 1)

        forward(g).wait_recv()
        unpack(sib_arrived, g, ROWS)
        total[...] = jnp.zeros_like(total)

        def hidden_chunk(i, c):
            cols = pl.ds(pl.multiple_of(i * FFC, FFC), FFC)
            hidden = jax.nn.gelu(dot(x_rows[...], win[:, cols])).astype(bf16)
            total[...] += dot(hidden, wout[cols, :])
            return c

        lax.fori_loop(0, win.shape[1] // FFC, hidden_chunk, 0)
        own_part[g] = total[0:ROWS].astype(bf16)
        send_part[g] = total[ROWS:2 * ROWS].astype(bf16)
        swap(g).start()
        return c

    lax.fori_loop(0, GROUPS, work, 0)
    finish(GROUPS - 1)

    def collect(g, c):
        pltpu.make_async_copy(group(ret_arrived, g), group(ret_arrived, g), r_recv.at[g]).wait()
        unpack(ret_arrived, g, 0)
        mask = (slot_col_ref[...] == g * ROWS + iota((tokens, ROWS), 1)).astype(bf16)
        token_total[...] += dot(mask, x_rows[0:ROWS])
        return c

    lax.fori_loop(0, GROUPS, collect, 0)

    layer_out = (tok[...].astype(f32) + gate_ref[...] * token_total[...]).astype(bf16)
    out_ref[...] = layer_out

    UR = 16
    row, at = iota((UR, tokens), 0), iota((UR, tokens), 1)
    first = jnp.where((row == 0) | (row == 2), 0, half)
    length = jnp.where(row == 2, clen[0], clen[1])
    start = jnp.where(row < 2, first, first + IMG_TOK)
    stop = first + IMG_TOK + jnp.where(row < 2, 0, length)
    pool = ((at >= start) & (at < stop) & (row < 4)).astype(bf16)
    row1 = iota((UR, 1), 0)
    count = jnp.where(row1 < 2, IMG_TOK, jnp.where(row1 == 2, clen[0], clen[1])).astype(f32)
    vectors = dot(pool, layer_out) / count
    squares = jnp.sum(vectors * vectors, axis=1, keepdims=True) + norm_eps
    unit = (vectors * lax.rsqrt(squares)).astype(bf16)
    gram = logit_scale * dot_nt(unit, unit)
    gram_row, gram_col = iota((UR, UR), 0), iota((UR, UR), 1)

    def pick(i):
        hit = (gram_row == i) & (gram_col == i + 2)
        return jnp.sum(jnp.sum(jnp.where(hit, gram, 0.0), axis=1, keepdims=True), axis=0, keepdims=True)

    stacked = jnp.concatenate([unit[:, j * LANES:(j + 1) * LANES] for j in range(CH)], axis=0)
    to = iota((2 * UR, 1), 0)
    inner = to % (2 * CH)
    source = (inner // 2) * UR + (to // (2 * CH)) * 2 + inner % 2
    select = (iota((2 * UR, CH * UR), 1) == source).astype(bf16)
    packed = dot(select, stacked).astype(bf16)
    units[0] = packed[0:UR]
    units[1] = packed[UR:2 * UR]

    def send_images(q, c):
        pltpu.make_async_remote_copy(
            src_ref=units.at[0], dst_ref=image_blocks.at[q], send_sem=g_send.at[0],
            recv_sem=g_recv.at[0], device_id=ring(offset(q)), device_id_type=MESH,
        ).start()
        return c

    def send_texts(m, c):
        pltpu.make_async_remote_copy(
            src_ref=units.at[1], dst_ref=text_blocks.at[m], send_sem=g_send.at[1],
            recv_sem=g_recv.at[1], device_id=in_plane(m), device_id_type=MESH,
        ).start()
        return c

    lax.fori_loop(0, Z - 1, send_images, 0)
    lax.fori_loop(1, PLANE, send_texts, 0)
    image_blocks[Z - 1] = packed[0:UR]
    text_blocks[0] = packed[UR:2 * UR]
    row_vec[...] = jnp.zeros_like(row_vec)
    col_vec[...] = jnp.zeros_like(col_vec)

    def others(ref, first, sem):
        part = ref.at[pl.ds(first, ref.shape[0] - 1)]
        return pltpu.make_async_copy(part, part, sem)

    def lay_rows(blocks, matrix, rows_ref, n):
        rows = dot(matrix[...], blocks[...].reshape(n * UR, LANES)).astype(bf16)
        for j in range(CH):
            rows_ref[:, j * LANES:(j + 1) * LANES] = rows[j * 2 * n:(j + 1) * 2 * n]

    others(text_blocks, 1, g_recv.at[1]).wait()
    lay_rows(text_blocks, unfold_p, text_rows, PLANE)
    others(image_blocks, 0, g_recv.at[0]).wait()
    lay_rows(image_blocks, unfold_z, image_rows, Z)
    by_image = jnp.exp(logit_scale * dot_nt(text_rows[...], image_rows[...]))
    row_vec[:, 0:2 * Z] = jnp.sum(by_image, axis=0, keepdims=True)
    by_text = jnp.exp(logit_scale * dot_nt(image_rows[...], text_rows[...]))
    col_vec[:, 0:2 * PLANE] = jnp.sum(by_text, axis=0, keepdims=True)

    def send_rows(q, c):
        pltpu.make_async_remote_copy(
            src_ref=row_vec, dst_ref=row_parts.at[q], send_sem=s_send.at[0],
            recv_sem=s_recv.at[0], device_id=ring(offset(q)), device_id_type=MESH,
        ).start()
        return c

    def send_cols(m, c):
        pltpu.make_async_remote_copy(
            src_ref=col_vec, dst_ref=col_parts.at[m], send_sem=s_send.at[1],
            recv_sem=s_recv.at[1], device_id=in_plane(m), device_id_type=MESH,
        ).start()
        return c

    lax.fori_loop(0, Z - 1, send_rows, 0)
    lax.fori_loop(1, PLANE, send_cols, 0)
    row_parts[Z - 1] = row_vec[...]
    col_parts[0] = col_vec[...]

    q = iota((Z, 1, LANES), 0)
    lane = iota((Z, 1, LANES), 2)
    back = jnp.where((q == 0) | (q == Z - 1), q, jnp.where(q % 2 == 1, q + 1, q - 1))
    m = iota((PLANE, 1, LANES), 0)
    mlane = iota((PLANE, 1, LANES), 2)
    mback = ((DP - m // CORES) % DP) * CORES + ((CORES - m % CORES) % CORES)

    def mine(parts, lanes, at):
        kept = jnp.where(lanes == at, parts, 0.0)
        return jnp.sum(jnp.sum(kept, axis=0), axis=1, keepdims=True)

    others(col_parts, 1, s_recv.at[1]).wait()
    col_total = [mine(col_parts[...], mlane, 2 * mback + i) for i in range(2)]
    others(row_parts, 0, s_recv.at[0]).wait()
    row_total = [mine(row_parts[...], lane, 2 * back + i) for i in range(2)]
    losses = [
        0.5 * (jnp.log(row_total[i]) - pick(i)) + 0.5 * (jnp.log(col_total[i]) - pick(i))
        for i in range(2)
    ]
    loss_ref[...] = jnp.where(iota((1, LANES), 1) == 0, losses[0], losses[1])

    def sent(part, sem):
        pltpu.make_async_copy(part, part, sem).wait()

    sent(out_blocks.at[pl.ds(0, Z - 1)], d_send)
    sent(ret_blocks.at[pl.ds(0, Z - 1)], r_send)

    def drain(g, c):
        forward(g).wait_send()
        swap(g).wait_send()
        return c

    lax.fori_loop(0, GROUPS, drain, 0)
    sent(image_blocks.at[pl.ds(0, Z - 1)], g_send.at[0])
    sent(text_blocks.at[pl.ds(1, PLANE - 1)], g_send.at[1])
    sent(row_parts.at[pl.ds(0, Z - 1)], s_send.at[0])
    sent(col_parts.at[pl.ds(1, PLANE - 1)], s_send.at[1])


def per_device(tokens, expert_ids, caption_len, router, expert_in, expert_out, *, cfg):
    pairs, seq, width = tokens.shape
    count = pairs * seq
    Z, DP, CAP, CH, GS, FFC = cfg
    PLANE = DP * CORES
    GROUPS = Z // GS
    BLK = CAP * CH
    ROWS = GS * CAP
    hidden = expert_in.shape[2]
    vmem = pl.BlockSpec(memory_space=pltpu.VMEM)
    dma = pltpu.SemaphoreType.DMA
    blocks = pltpu.VMEM((Z, BLK, LANES), bf16)
    parts = pltpu.VMEM((GROUPS, ROWS, width), bf16)
    out, loss = pl.pallas_call(
        functools.partial(kernel, cfg),
        out_shape=(
            jax.ShapeDtypeStruct((count, width), bf16),
            jax.ShapeDtypeStruct((1, LANES), f32),
        ),
        in_specs=[
            vmem, vmem, pl.BlockSpec(memory_space=pltpu.SMEM), vmem,
            pl.BlockSpec(memory_space=pl.ANY), pl.BlockSpec(memory_space=pl.ANY),
        ],
        out_specs=(vmem, vmem),
        scratch_shapes=[
            pltpu.VMEM((width, hidden), bf16),
            pltpu.VMEM((hidden, width), bf16),
            pltpu.VMEM((GS * BLK, GS * BLK), bf16),
            pltpu.VMEM((GS * BLK, GS * BLK), bf16),
            pltpu.VMEM((Z * 16, Z * 16), bf16),
            pltpu.VMEM((PLANE * 16, PLANE * 16), bf16),
            pltpu.VMEM((count, 1), jnp.int32),
            pltpu.VMEM((count, 1), f32),
            blocks, blocks, blocks,
            pltpu.VMEM((2 * ROWS, width), bf16),
            pltpu.VMEM((2 * ROWS, width), f32),
            parts, parts, parts, blocks, blocks,
            pltpu.VMEM((count, width), f32),
            pltpu.VMEM((2, 16, LANES), bf16),
            pltpu.VMEM((Z, 16, LANES), bf16),
            pltpu.VMEM((PLANE, 16, LANES), bf16),
            pltpu.VMEM((2 * Z, width), bf16),
            pltpu.VMEM((2 * PLANE, width), bf16),
            pltpu.VMEM((1, LANES), f32),
            pltpu.VMEM((1, LANES), f32),
            pltpu.VMEM((Z, 1, LANES), f32),
            pltpu.VMEM((PLANE, 1, LANES), f32),
            dma((2,)), dma, dma((GROUPS,)), dma((GROUPS,)), dma((GROUPS,)),
            dma((GROUPS,)), dma((GROUPS,)), dma, dma((GROUPS,)),
            dma((2,)), dma((2,)), dma((2,)), dma((2,)),
        ],
        compiler_params=pltpu.CompilerParams(
            collective_id=0, has_side_effects=True, vmem_limit_bytes=40 << 20
        ),
        cost_estimate=pl.CostEstimate(
            flops=8 * Z * CAP * width * hidden, bytes_accessed=4 * width * hidden, transcendentals=0
        ),
        name="expert_contrast",
    )(
        tokens.reshape(count, width),
        jnp.swapaxes(expert_ids, 1, 2),
        caption_len,
        router.T,
        expert_in,
        expert_out,
    )
    return out.reshape(pairs, seq, width), loss[0, :pairs]


def solution(mesh, cap=6, group=8, ff_chunk=512):
    cfg = (mesh.shape["expert"] // CORES, mesh.shape["dp"], cap, 8, group, ff_chunk)
    return jax.shard_map(
        functools.partial(per_device, cfg=cfg),
        mesh=mesh,
        in_specs=(
            P(("dp", "expert"), None, None),
            P(("dp", "expert"), None, None),
            P(("dp", "expert")),
            P(),
            P("expert", None, None),
            P("expert", None, None),
        ),
        out_specs=(P(("dp", "expert"), None, None), P(("dp", "expert"))),
        check_vma=False,
    )
```

```python
import functools

import jax
import jax.numpy as jnp
from jax import lax
from jax.experimental import pallas as pl
from jax.experimental.pallas import tpu as pltpu
from jax.sharding import PartitionSpec as P

IMG_TOK = 48
LANES = 128
CORES = 2
logit_scale = 20.0
norm_eps = 1e-06
MESH = pl.DeviceIdType.MESH
bf16 = jnp.bfloat16
f32 = jnp.float32


def iota(shape, axis):
    return lax.broadcasted_iota(jnp.int32, shape, axis)


def dot(a, b):
    return jnp.dot(a, b, preferred_element_type=f32)


def dot_nt(a, b):
    return lax.dot_general(a, b, (((1,), (1,)), ((), ())), preferred_element_type=f32)


def chunk_major(blocks, chunks, rows):
    size = blocks * chunks * rows
    to = iota((size, 1), 0)
    chunk, rest = to // (blocks * rows), to % (blocks * rows)
    source = (rest // rows) * (chunks * rows) + chunk * rows + rest % rows
    return (iota((size, size), 1) == source).astype(bf16)


def block_major(blocks, chunks, rows):
    size = blocks * chunks * rows
    to = iota((size, 1), 0)
    block, rest = to // (chunks * rows), to % (chunks * rows)
    source = (rest // rows) * (blocks * rows) + block * rows + rest % rows
    return (iota((size, size), 1) == source).astype(bf16)


def kernel(
    cfg, tok_hbm, ids_hbm, clen_hbm, router_hbm, win_hbm, wout_hbm, out_hbm, loss_ref,
    tok, ids, clen, router_t, out_ref, win, wout, unfold, fold, unfold_z, unfold_p, slot_col_ref, gate_ref,
    out_blocks, arrived, sib_arrived, x_rows, total,
    own_part, send_part, sib_part, ret_blocks, ret_arrived, token_total,
    units, image_blocks, text_blocks, image_rows, text_rows,
    row_vec, col_vec, row_parts, col_parts,
    w_sem, far_sem, d_send, d_recv, f_send, f_recv, p_send, p_recv, r_send, r_recv,
    g_send, g_recv, s_send, s_recv,
):
    Z, DP, CAP, CH, GS, FFC = cfg
    PLANE = DP * CORES
    GROUPS = Z // GS
    BLK = CAP * CH
    ROWS = GS * CAP
    tokens = tok.shape[0]
    half = tokens // 2
    dp = lax.axis_index("dp")
    ex = lax.axis_index("expert")
    z = ex // CORES
    core = ex % CORES

    def ring(k):
        return {"dp": dp, "expert": lax.rem(z + k, Z) * CORES + core}

    def in_plane(m):
        return {
            "dp": lax.rem(dp + m // CORES, DP),
            "expert": z * CORES + lax.rem(core + m % CORES, CORES),
        }

    sibling = {"dp": dp, "expert": z * CORES + (1 - core)}

    def offset(q):
        return jnp.where(q % 2 == 1, Z // 2 - (q + 1) // 2, lax.rem(q // 2 + Z // 2, Z))

    barrier = pltpu.get_barrier_semaphore()

    def greet_ring(k, c):
        pl.semaphore_signal(barrier, inc=1, device_id=ring(k), device_id_type=MESH)
        return c

    def greet_plane(m, c):
        pl.semaphore_signal(barrier, inc=1, device_id=in_plane(m), device_id_type=MESH)
        return c

    NEAR = Z // 4
    load_ids = pltpu.make_async_copy(ids_hbm, ids, w_sem.at[0])
    load_tok = pltpu.make_async_copy(tok_hbm, tok, w_sem.at[1])
    load_router = pltpu.make_async_copy(router_hbm, router_t, w_sem.at[2])
    load_clen = pltpu.make_async_copy(clen_hbm, clen, w_sem.at[3])
    load_in = pltpu.make_async_copy(win_hbm.at[0], win, w_sem.at[4])
    load_out = pltpu.make_async_copy(wout_hbm.at[0], wout, w_sem.at[5])
    load_ids.start()
    load_tok.start()
    lax.fori_loop(1, NEAR + 1, greet_ring, 0)
    lax.fori_loop(Z - NEAR, Z, greet_ring, 0)
    lax.fori_loop(1, PLANE, greet_plane, 0)
    load_router.start()
    load_clen.start()
    load_in.start()
    load_out.start()

    fold[...] = block_major(GS, CH, CAP)
    load_ids.wait()
    ids_row = jnp.concatenate([ids[0], ids[1]], axis=1)
    eye = iota((tokens, tokens), 0) == iota((tokens, tokens), 1)
    onehot_t = iota((Z, tokens), 0) == ids_row
    upto = (iota((tokens, tokens), 0) <= iota((tokens, tokens), 1)).astype(bf16)
    running = dot(onehot_t.astype(bf16), upto)
    position = jnp.sum(jnp.where(onehot_t, running, 0.0), axis=0, keepdims=True).astype(jnp.int32) - 1
    ahead = ids_row - z
    ahead = jnp.where(ahead < 0, ahead + Z, ahead)
    signed = jnp.where(ahead > Z // 2, ahead - Z, ahead)
    away = jnp.abs(signed)
    order = 2 * (Z // 2 - away) - jnp.where((signed >= 0) & (away < Z // 2), 1, 0)
    slot_row = order * CAP + position
    slot_col_ref[...] = jnp.sum(jnp.where(eye, slot_row.astype(f32), 0.0), axis=1, keepdims=True).astype(jnp.int32)
    ids_col = jnp.sum(jnp.where(eye, ids_row.astype(f32), 0.0), axis=1, keepdims=True).astype(jnp.int32)

    load_tok.wait()

    def pack(i, c):
        g = GROUPS - 1 - i
        mask = (slot_row == g * ROWS + iota((ROWS, tokens), 0)).astype(bf16)
        rows = dot(mask, tok[...]).astype(bf16)
        stacked = jnp.concatenate([rows[:, j * LANES:(j + 1) * LANES] for j in range(CH)], axis=0)
        out_blocks[pl.ds(g * GS, GS)] = dot(fold[...], stacked).astype(bf16).reshape(GS, BLK, LANES)
        return c

    lax.fori_loop(0, GROUPS, pack, 0)

    def send_out(q, c):
        pltpu.make_async_remote_copy(
            src_ref=out_blocks.at[q], dst_ref=arrived.at[q], send_sem=d_send,
            recv_sem=d_recv.at[q // GS], device_id=ring(offset(q)), device_id_type=MESH,
        ).start()
        return c

    pl.semaphore_wait(barrier, 2 * NEAR + PLANE - 1)
    for end in (NEAR, Z - NEAR):
        pl.semaphore_signal(far_sem, inc=1, device_id=ring(end), device_id_type=MESH)
    lax.fori_loop(Z // 2 - 1, Z - 1, send_out, 0)
    pltpu.make_async_copy(out_blocks.at[Z - 1], arrived.at[Z - 1], d_recv.at[GROUPS - 1]).start()
    unfold[...] = chunk_major(GS, CH, CAP)
    pl.semaphore_wait(far_sem, 2)
    lax.fori_loop(0, Z // 2 - 1, send_out, 0)

    load_router.wait()
    load_clen.wait()
    logits = dot_nt(tok[...], router_t[...])
    onehot = iota((tokens, Z), 1) == ids_col
    gate_ref[...] = jax.nn.sigmoid(jnp.sum(jnp.where(onehot, logits, 0.0), axis=1, keepdims=True))
    token_total[...] = jnp.zeros_like(token_total)
    unfold_z[...] = chunk_major(Z, CH, 2)
    unfold_p[...] = chunk_major(PLANE, CH, 2)
    load_in.wait()
    load_out.wait()

    def group(ref, g):
        return ref.at[pl.ds(g * GS, GS)]

    def unpack(ref, g, base):
        blocks = ref[pl.ds(g * GS, GS)].reshape(GS * BLK, LANES)
        rows = dot(unfold[...], blocks).astype(bf16)
        for j in range(CH):
            x_rows[base:base + ROWS, j * LANES:(j + 1) * LANES] = rows[j * ROWS:(j + 1) * ROWS]

    def forward(g):
        return pltpu.make_async_remote_copy(
            src_ref=group(arrived, g), dst_ref=group(sib_arrived, g), send_sem=f_send.at[g],
            recv_sem=f_recv.at[g], device_id=sibling, device_id_type=MESH,
        )

    def swap(g):
        return pltpu.make_async_remote_copy(
            src_ref=send_part.at[g], dst_ref=sib_part.at[g], send_sem=p_send.at[g],
            recv_sem=p_recv.at[g], device_id=sibling, device_id_type=MESH,
        )

    def finish(g):
        swap(g).wait_recv()
        both = (own_part[g].astype(f32) + sib_part[g].astype(f32)).astype(bf16)
        stacked = jnp.concatenate([both[:, j * LANES:(j + 1) * LANES] for j in range(CH)], axis=0)
        ret_blocks[pl.ds(g * GS, GS)] = dot(fold[...], stacked).astype(bf16).reshape(GS, BLK, LANES)

    def send_group(g):
        def send_back(i, c):
            q = g * GS + i
            pltpu.make_async_remote_copy(
                src_ref=ret_blocks.at[q], dst_ref=ret_arrived.at[q], send_sem=r_send,
                recv_sem=r_recv.at[g], device_id=ring(Z - offset(q)), device_id_type=MESH,
            ).start()
            return c

        lax.fori_loop(0, jnp.where(g == GROUPS - 1, GS - 1, GS), send_back, 0)

        @pl.when(g == GROUPS - 1)
        def _():
            pltpu.make_async_copy(ret_blocks.at[Z - 1], ret_arrived.at[Z - 1], r_recv.at[g]).start()

    def place(i):
        return jnp.where(i < GROUPS // 2, GROUPS - 1 - i, i - GROUPS // 2)

    def work(i, c):
        g = place(i)
        pltpu.make_async_copy(group(arrived, g), group(arrived, g), d_recv.at[g]).wait()
        forward(g).start()
        unpack(arrived, g, 0)

        @pl.when(i > 0)
        def _():
            finish(place(i - 1))

        @pl.when(i > GROUPS // 2)
        def _():
            send_group(place(i - 1))

        forward(g).wait_recv()
        unpack(sib_arrived, g, ROWS)
        total[...] = jnp.zeros_like(total)

        def hidden_chunk(i, c):
            cols = pl.ds(pl.multiple_of(i * FFC, FFC), FFC)
            hidden = jax.nn.gelu(dot(x_rows[...], win[:, cols])).astype(bf16)
            total[...] += dot(hidden, wout[cols, :])
            return c

        lax.fori_loop(0, win.shape[1] // FFC, hidden_chunk, 0)
        own_part[g] = total[0:ROWS].astype(bf16)
        send_part[g] = total[ROWS:2 * ROWS].astype(bf16)
        swap(g).start()
        return c

    lax.fori_loop(0, GROUPS, work, 0)
    finish(GROUPS // 2 - 1)

    def send_rest(g, c):
        send_group(g)
        return c

    lax.fori_loop(GROUPS // 2 - 1, GROUPS, send_rest, 0)

    def collect(g, c):
        pltpu.make_async_copy(group(ret_arrived, g), group(ret_arrived, g), r_recv.at[g]).wait()
        unpack(ret_arrived, g, 0)
        mask = (slot_col_ref[...] == g * ROWS + iota((tokens, ROWS), 1)).astype(bf16)
        token_total[...] += dot(mask, x_rows[0:ROWS])
        return c

    lax.fori_loop(0, GROUPS, collect, 0)

    layer_out = (tok[...].astype(f32) + gate_ref[...] * token_total[...]).astype(bf16)
    out_ref[...] = layer_out
    store = pltpu.make_async_copy(out_ref, out_hbm, w_sem.at[0])
    store.start()

    UR = 16
    row, at = iota((UR, tokens), 0), iota((UR, tokens), 1)
    first = jnp.where((row == 0) | (row == 2), 0, half)
    length = jnp.where(row == 2, clen[0], clen[1])
    start = jnp.where(row < 2, first, first + IMG_TOK)
    stop = first + IMG_TOK + jnp.where(row < 2, 0, length)
    pool = ((at >= start) & (at < stop) & (row < 4)).astype(bf16)
    row1 = iota((UR, 1), 0)
    count = jnp.where(row1 < 2, IMG_TOK, jnp.where(row1 == 2, clen[0], clen[1])).astype(f32)
    vectors = dot(pool, layer_out) / count
    squares = jnp.sum(vectors * vectors, axis=1, keepdims=True) + norm_eps
    unit = (vectors * lax.rsqrt(squares)).astype(bf16)
    gram = logit_scale * dot_nt(unit, unit)
    gram_row, gram_col = iota((UR, UR), 0), iota((UR, UR), 1)

    def pick(i):
        hit = (gram_row == i) & (gram_col == i + 2)
        return jnp.sum(jnp.sum(jnp.where(hit, gram, 0.0), axis=1, keepdims=True), axis=0, keepdims=True)

    stacked = jnp.concatenate([unit[:, j * LANES:(j + 1) * LANES] for j in range(CH)], axis=0)
    to = iota((2 * UR, 1), 0)
    inner = to % (2 * CH)
    source = (inner // 2) * UR + (to // (2 * CH)) * 2 + inner % 2
    select = (iota((2 * UR, CH * UR), 1) == source).astype(bf16)
    packed = dot(select, stacked).astype(bf16)
    units[0] = packed[0:UR]
    units[1] = packed[UR:2 * UR]

    def send_images(q, c):
        pltpu.make_async_remote_copy(
            src_ref=units.at[0], dst_ref=image_blocks.at[q], send_sem=g_send.at[0],
            recv_sem=g_recv.at[0], device_id=ring(offset(q)), device_id_type=MESH,
        ).start()
        return c

    def send_texts(m, c):
        pltpu.make_async_remote_copy(
            src_ref=units.at[1], dst_ref=text_blocks.at[m], send_sem=g_send.at[1],
            recv_sem=g_recv.at[1], device_id=in_plane(m), device_id_type=MESH,
        ).start()
        return c

    lax.fori_loop(0, Z - 1, send_images, 0)
    lax.fori_loop(1, PLANE, send_texts, 0)
    image_blocks[Z - 1] = packed[0:UR]
    text_blocks[0] = packed[UR:2 * UR]
    row_vec[...] = jnp.zeros_like(row_vec)
    col_vec[...] = jnp.zeros_like(col_vec)

    def others(ref, first, sem):
        part = ref.at[pl.ds(first, ref.shape[0] - 1)]
        return pltpu.make_async_copy(part, part, sem)

    def lay_rows(blocks, matrix, rows_ref, n):
        rows = dot(matrix[...], blocks[...].reshape(n * UR, LANES)).astype(bf16)
        for j in range(CH):
            rows_ref[:, j * LANES:(j + 1) * LANES] = rows[j * 2 * n:(j + 1) * 2 * n]

    others(text_blocks, 1, g_recv.at[1]).wait()
    lay_rows(text_blocks, unfold_p, text_rows, PLANE)
    others(image_blocks, 0, g_recv.at[0]).wait()
    lay_rows(image_blocks, unfold_z, image_rows, Z)
    by_image = jnp.exp(logit_scale * dot_nt(text_rows[...], image_rows[...]))
    row_vec[:, 0:2 * Z] = jnp.sum(by_image, axis=0, keepdims=True)
    by_text = jnp.exp(logit_scale * dot_nt(image_rows[...], text_rows[...]))
    col_vec[:, 0:2 * PLANE] = jnp.sum(by_text, axis=0, keepdims=True)

    def send_rows(q, c):
        pltpu.make_async_remote_copy(
            src_ref=row_vec, dst_ref=row_parts.at[q], send_sem=s_send.at[0],
            recv_sem=s_recv.at[0], device_id=ring(offset(q)), device_id_type=MESH,
        ).start()
        return c

    def send_cols(m, c):
        pltpu.make_async_remote_copy(
            src_ref=col_vec, dst_ref=col_parts.at[m], send_sem=s_send.at[1],
            recv_sem=s_recv.at[1], device_id=in_plane(m), device_id_type=MESH,
        ).start()
        return c

    lax.fori_loop(0, Z - 1, send_rows, 0)
    lax.fori_loop(1, PLANE, send_cols, 0)
    row_parts[Z - 1] = row_vec[...]
    col_parts[0] = col_vec[...]

    q = iota((Z, 1, LANES), 0)
    lane = iota((Z, 1, LANES), 2)
    back = jnp.where((q == 0) | (q == Z - 1), q, jnp.where(q % 2 == 1, q + 1, q - 1))
    m = iota((PLANE, 1, LANES), 0)
    mlane = iota((PLANE, 1, LANES), 2)
    mback = ((DP - m // CORES) % DP) * CORES + ((CORES - m % CORES) % CORES)

    def mine(parts, lanes, at):
        kept = jnp.where(lanes == at, parts, 0.0)
        return jnp.sum(jnp.sum(kept, axis=0), axis=1, keepdims=True)

    others(col_parts, 1, s_recv.at[1]).wait()
    col_total = [mine(col_parts[...], mlane, 2 * mback + i) for i in range(2)]
    others(row_parts, 0, s_recv.at[0]).wait()
    row_total = [mine(row_parts[...], lane, 2 * back + i) for i in range(2)]
    losses = [
        0.5 * (jnp.log(row_total[i]) - pick(i)) + 0.5 * (jnp.log(col_total[i]) - pick(i))
        for i in range(2)
    ]
    loss_ref[...] = jnp.where(iota((1, LANES), 1) == 0, losses[0], losses[1])

    store.wait()
    def sent(part, sem):
        pltpu.make_async_copy(part, part, sem).wait()

    sent(out_blocks.at[pl.ds(0, Z - 1)], d_send)
    sent(ret_blocks.at[pl.ds(0, Z - 1)], r_send)

    def drain(g, c):
        forward(g).wait_send()
        swap(g).wait_send()
        return c

    lax.fori_loop(0, GROUPS, drain, 0)
    sent(image_blocks.at[pl.ds(0, Z - 1)], g_send.at[0])
    sent(text_blocks.at[pl.ds(1, PLANE - 1)], g_send.at[1])
    sent(row_parts.at[pl.ds(0, Z - 1)], s_send.at[0])
    sent(col_parts.at[pl.ds(1, PLANE - 1)], s_send.at[1])


def per_device(tokens, expert_ids, caption_len, router, expert_in, expert_out, *, cfg):
    pairs, seq, width = tokens.shape
    count = pairs * seq
    Z, DP, CAP, CH, GS, FFC = cfg
    PLANE = DP * CORES
    GROUPS = Z // GS
    BLK = CAP * CH
    ROWS = GS * CAP
    hidden = expert_in.shape[2]
    vmem = pl.BlockSpec(memory_space=pltpu.VMEM)
    hbm = pl.BlockSpec(memory_space=pltpu.HBM)
    dma = pltpu.SemaphoreType.DMA
    blocks = pltpu.VMEM((Z, BLK, LANES), bf16)
    parts = pltpu.VMEM((GROUPS, ROWS, width), bf16)
    out, loss = pl.pallas_call(
        functools.partial(kernel, cfg),
        out_shape=(
            jax.ShapeDtypeStruct((count, width), bf16),
            jax.ShapeDtypeStruct((1, LANES), f32),
        ),
        in_specs=[
            hbm, hbm, hbm, hbm, hbm, hbm,
        ],
        out_specs=(hbm, vmem),
        scratch_shapes=[
            pltpu.VMEM((count, width), bf16),
            pltpu.VMEM((pairs, 1, seq), jnp.int32),
            pltpu.SMEM((pairs,), jnp.int32),
            pltpu.VMEM((Z, width), bf16),
            pltpu.VMEM((count, width), bf16),
            pltpu.VMEM((width, hidden), bf16),
            pltpu.VMEM((hidden, width), bf16),
            pltpu.VMEM((GS * BLK, GS * BLK), bf16),
            pltpu.VMEM((GS * BLK, GS * BLK), bf16),
            pltpu.VMEM((Z * 16, Z * 16), bf16),
            pltpu.VMEM((PLANE * 16, PLANE * 16), bf16),
            pltpu.VMEM((count, 1), jnp.int32),
            pltpu.VMEM((count, 1), f32),
            blocks, blocks, blocks,
            pltpu.VMEM((2 * ROWS, width), bf16),
            pltpu.VMEM((2 * ROWS, width), f32),
            parts, parts, parts, blocks, blocks,
            pltpu.VMEM((count, width), f32),
            pltpu.VMEM((2, 16, LANES), bf16),
            pltpu.VMEM((Z, 16, LANES), bf16),
            pltpu.VMEM((PLANE, 16, LANES), bf16),
            pltpu.VMEM((2 * Z, width), bf16),
            pltpu.VMEM((2 * PLANE, width), bf16),
            pltpu.VMEM((1, LANES), f32),
            pltpu.VMEM((1, LANES), f32),
            pltpu.VMEM((Z, 1, LANES), f32),
            pltpu.VMEM((PLANE, 1, LANES), f32),
            dma((6,)), pltpu.SemaphoreType.REGULAR, dma, dma((GROUPS,)), dma((GROUPS,)), dma((GROUPS,)),
            dma((GROUPS,)), dma((GROUPS,)), dma, dma((GROUPS,)),
            dma((2,)), dma((2,)), dma((2,)), dma((2,)),
        ],
        compiler_params=pltpu.CompilerParams(
            collective_id=0, has_side_effects=True, vmem_limit_bytes=64 << 20
        ),
        cost_estimate=pl.CostEstimate(
            flops=8 * Z * CAP * width * hidden, bytes_accessed=4 * width * hidden, transcendentals=0
        ),
        name="expert_contrast",
    )(
        tokens.reshape(count, width),
        jnp.swapaxes(expert_ids, 1, 2),
        caption_len,
        router.T,
        expert_in,
        expert_out,
    )
    return out.reshape(pairs, seq, width), loss[0, :pairs]


def solution(mesh, cap=6, group=8, ff_chunk=512):
    cfg = (mesh.shape["expert"] // CORES, mesh.shape["dp"], cap, 8, group, ff_chunk)
    return jax.shard_map(
        functools.partial(per_device, cfg=cfg),
        mesh=mesh,
        in_specs=(
            P(("dp", "expert"), None, None),
            P(("dp", "expert"), None, None),
            P(("dp", "expert")),
            P(),
            P("expert", None, None),
            P("expert", None, None),
        ),
        out_specs=(P(("dp", "expert"), None, None), P(("dp", "expert"))),
        check_vma=False,
    )
```

```python
import functools

import jax
import jax.numpy as jnp
from jax import lax
from jax.experimental import pallas as pl
from jax.experimental.pallas import tpu as pltpu
from jax.sharding import PartitionSpec as P

IMG_TOK = 48
LANES = 128
CORES = 2
logit_scale = 20.0
norm_eps = 1e-06
MESH = pl.DeviceIdType.MESH
bf16 = jnp.bfloat16
f32 = jnp.float32


def iota(shape, axis):
    return lax.broadcasted_iota(jnp.int32, shape, axis)


def dot(a, b):
    return jnp.dot(a, b, preferred_element_type=f32)


def dot_nt(a, b):
    return lax.dot_general(a, b, (((1,), (1,)), ((), ())), preferred_element_type=f32)


def chunk_major(blocks, chunks, rows):
    size = blocks * chunks * rows
    to = iota((size, 1), 0)
    chunk, rest = to // (blocks * rows), to % (blocks * rows)
    source = (rest // rows) * (chunks * rows) + chunk * rows + rest % rows
    return (iota((size, size), 1) == source).astype(bf16)


def block_major(blocks, chunks, rows):
    size = blocks * chunks * rows
    to = iota((size, 1), 0)
    block, rest = to // (chunks * rows), to % (chunks * rows)
    source = (rest // rows) * (blocks * rows) + block * rows + rest % rows
    return (iota((size, size), 1) == source).astype(bf16)


def plane_shape(DP):
    XN = 1
    while 4 * XN * XN <= DP:
        XN *= 2
    return XN, DP // XN


def meeting(Z):
    if Z % 32:
        return Z, 1, []
    images, captions = 8, 5
    seen, repeated = set(), []
    for i in range(images):
        for j in range(captions):
            apart = (image_offset(Z, i) - caption_offset(Z, j)) % Z
            if apart in seen:
                repeated.append((i, j))
            seen.add(apart)
    assert len(seen) == Z
    return images, captions, repeated


def image_offset(Z, i):
    if Z % 32:
        return i
    return (Z // 4 - i // 2) * (1 - 2 * (i % 2))


def caption_offset(Z, j):
    if Z % 32:
        return 0 * j
    size = Z // 4 - (j - 1) // 2 * (Z // 8)
    return (1 - (j == 0)) * size * (1 - 2 * (j % 2))


def kernel(
    cfg, tok_hbm, ids_hbm, clen_hbm, router_hbm, win_hbm, wout_hbm, out_hbm, loss_ref,
    tok, ids, clen, router_t, out_ref, win, wout, unfold, fold, unfold_z, unfold_p, slot_col_ref, gate_ref,
    out_blocks, arrived, sib_arrived, x_rows, total,
    own_part, send_part, sib_part, ret_blocks, ret_arrived, token_total,
    units, image_blocks, text_blocks, image_rows, text_rows, once,
    row_vec, col_vec, row_parts, col_parts,
    w_sem, far_sem, d_send, d_recv, f_send, f_recv, p_send, p_recv, r_send, r_recv,
    g_send, g_recv, h_send, h_recv, s_send, s_recv,
):
    Z, DP, CAP, CH, GS, FFC = cfg
    XN, YN = plane_shape(DP)
    GROUPS = Z // GS
    BLK = CAP * CH
    ROWS = GS * CAP
    NA, NB, repeated = meeting(Z)
    NI, NT = XN * NA, YN * CORES * NB
    tokens = tok.shape[0]
    half = tokens // 2
    dp = lax.axis_index("dp")
    ex = lax.axis_index("expert")
    z = ex // CORES
    core = ex % CORES

    def ring(k):
        return {"dp": dp, "expert": lax.rem(z + k, Z) * CORES + core}

    x, y = dp // YN, dp % YN

    def along_x(dx, dz=0):
        return {
            "dp": lax.rem(x + dx, XN) * YN + y,
            "expert": lax.rem(z + dz + Z, Z) * CORES + core,
        }

    def along_y(m, dz=0):
        return {
            "dp": x * YN + lax.rem(y + m // CORES, YN),
            "expert": lax.rem(z + dz + Z, Z) * CORES + lax.rem(core + m % CORES, CORES),
        }

    sibling = {"dp": dp, "expert": z * CORES + (1 - core)}

    def offset(q):
        return jnp.where(q % 2 == 1, Z // 2 - (q + 1) // 2, lax.rem(q // 2 + Z // 2, Z))

    barrier = pltpu.get_barrier_semaphore()

    def greet_ring(k, c):
        pl.semaphore_signal(barrier, inc=1, device_id=ring(k), device_id_type=MESH)
        return c

    def greet_x(m, c):
        pl.semaphore_signal(barrier, inc=1, device_id=along_x(m), device_id_type=MESH)
        return c

    def greet_y(m, c):
        pl.semaphore_signal(barrier, inc=1, device_id=along_y(m), device_id_type=MESH)
        return c

    NEAR = Z // 8
    load_ids = pltpu.make_async_copy(ids_hbm, ids, w_sem.at[0])
    load_tok = pltpu.make_async_copy(tok_hbm, tok, w_sem.at[1])
    load_router = pltpu.make_async_copy(router_hbm, router_t, w_sem.at[2])
    load_clen = pltpu.make_async_copy(clen_hbm, clen, w_sem.at[3])
    load_in = pltpu.make_async_copy(win_hbm.at[0], win, w_sem.at[4])
    load_out = pltpu.make_async_copy(wout_hbm.at[0], wout, w_sem.at[5])
    load_ids.start()
    load_tok.start()
    lax.fori_loop(1, NEAR + 1, greet_ring, 0)
    lax.fori_loop(Z - NEAR, Z, greet_ring, 0)
    lax.fori_loop(1, XN, greet_x, 0)
    lax.fori_loop(1, YN * CORES, greet_y, 0)
    load_router.start()
    load_clen.start()
    load_in.start()
    load_out.start()

    fold[...] = block_major(GS, CH, CAP)
    load_ids.wait()
    ids_row = jnp.concatenate([ids[0], ids[1]], axis=1)
    eye = iota((tokens, tokens), 0) == iota((tokens, tokens), 1)
    onehot_t = iota((Z, tokens), 0) == ids_row
    upto = (iota((tokens, tokens), 0) <= iota((tokens, tokens), 1)).astype(bf16)
    running = dot(onehot_t.astype(bf16), upto)
    position = jnp.sum(jnp.where(onehot_t, running, 0.0), axis=0, keepdims=True).astype(jnp.int32) - 1
    ahead = ids_row - z
    ahead = jnp.where(ahead < 0, ahead + Z, ahead)
    signed = jnp.where(ahead > Z // 2, ahead - Z, ahead)
    away = jnp.abs(signed)
    order = 2 * (Z // 2 - away) - jnp.where((signed >= 0) & (away < Z // 2), 1, 0)
    slot_row = order * CAP + position
    slot_col_ref[...] = jnp.sum(jnp.where(eye, slot_row.astype(f32), 0.0), axis=1, keepdims=True).astype(jnp.int32)
    ids_col = jnp.sum(jnp.where(eye, ids_row.astype(f32), 0.0), axis=1, keepdims=True).astype(jnp.int32)

    load_tok.wait()

    def pack(i, c):
        g = GROUPS - 1 - i
        mask = (slot_row == g * ROWS + iota((ROWS, tokens), 0)).astype(bf16)
        rows = dot(mask, tok[...]).astype(bf16)
        stacked = jnp.concatenate([rows[:, j * LANES:(j + 1) * LANES] for j in range(CH)], axis=0)
        out_blocks[pl.ds(g * GS, GS)] = dot(fold[...], stacked).astype(bf16).reshape(GS, BLK, LANES)
        return c

    lax.fori_loop(0, GROUPS, pack, 0)

    def send_out(q, c):
        pltpu.make_async_remote_copy(
            src_ref=out_blocks.at[q], dst_ref=arrived.at[q], send_sem=d_send.at[q // GS],
            recv_sem=d_recv.at[q // GS], device_id=ring(offset(q)), device_id_type=MESH,
        ).start()
        return c

    def tell(step, distance):
        for end in (distance, Z - distance):
            pl.semaphore_signal(far_sem.at[step], inc=1, device_id=ring(end), device_id_type=MESH)

    pl.semaphore_wait(barrier, 2 * NEAR + XN - 1 + YN * CORES - 1)
    tell(0, NEAR)
    lax.fori_loop(Z * 3 // 4 - 1, Z - 1, send_out, 0)
    pltpu.make_async_copy(out_blocks.at[Z - 1], arrived.at[Z - 1], d_recv.at[GROUPS - 1]).start()
    unfold[...] = chunk_major(GS, CH, CAP)
    pl.semaphore_wait(far_sem.at[0], 2)
    tell(1, 2 * NEAR)
    lax.fori_loop(Z // 2 - 1, Z * 3 // 4 - 1, send_out, 0)
    pl.semaphore_wait(far_sem.at[1], 2)
    lax.fori_loop(0, GS, send_out, 0)

    load_router.wait()
    load_clen.wait()
    logits = dot_nt(tok[...], router_t[...])
    onehot = iota((tokens, Z), 1) == ids_col
    gate_ref[...] = jax.nn.sigmoid(jnp.sum(jnp.where(onehot, logits, 0.0), axis=1, keepdims=True))
    token_total[...] = jnp.zeros_like(token_total)
    unfold_z[...] = chunk_major(NI, CH, 2)
    unfold_p[...] = chunk_major(NT, CH, 2)
    image_at, caption_at = iota((2 * NI, 2 * NT), 0) // 2 % NA, iota((2 * NI, 2 * NT), 1) // 2 % NB
    kept = jnp.ones((2 * NI, 2 * NT), f32)
    for i, j in repeated:
        kept = jnp.where((image_at == i) & (caption_at == j), 0.0, kept)
    once[...] = kept
    load_in.wait()
    load_out.wait()

    def group(ref, g):
        return ref.at[pl.ds(g * GS, GS)]

    def unpack(ref, g, base):
        blocks = ref[pl.ds(g * GS, GS)].reshape(GS * BLK, LANES)
        rows = dot(unfold[...], blocks).astype(bf16)
        for j in range(CH):
            x_rows[base:base + ROWS, j * LANES:(j + 1) * LANES] = rows[j * ROWS:(j + 1) * ROWS]

    def forward(g):
        return pltpu.make_async_remote_copy(
            src_ref=group(arrived, g), dst_ref=group(sib_arrived, g), send_sem=f_send.at[g],
            recv_sem=f_recv.at[g], device_id=sibling, device_id_type=MESH,
        )

    def swap(g):
        return pltpu.make_async_remote_copy(
            src_ref=send_part.at[g], dst_ref=sib_part.at[g], send_sem=p_send.at[g],
            recv_sem=p_recv.at[g], device_id=sibling, device_id_type=MESH,
        )

    def finish(g):
        swap(g).wait_recv()
        both = (own_part[g].astype(f32) + sib_part[g].astype(f32)).astype(bf16)
        stacked = jnp.concatenate([both[:, j * LANES:(j + 1) * LANES] for j in range(CH)], axis=0)
        ret_blocks[pl.ds(g * GS, GS)] = dot(fold[...], stacked).astype(bf16).reshape(GS, BLK, LANES)

    def send_group(g):
        def send_back(i, c):
            q = g * GS + i
            pltpu.make_async_remote_copy(
                src_ref=ret_blocks.at[q], dst_ref=ret_arrived.at[q], send_sem=r_send,
                recv_sem=r_recv.at[g], device_id=ring(Z - offset(q)), device_id_type=MESH,
            ).start()
            return c

        lax.fori_loop(0, jnp.where(g == GROUPS - 1, GS - 1, GS), send_back, 0)

        @pl.when(g == GROUPS - 1)
        def _():
            pltpu.make_async_copy(ret_blocks.at[Z - 1], ret_arrived.at[Z - 1], r_recv.at[g]).start()

    def place(i):
        return jnp.where(i < GROUPS // 2, GROUPS - 1 - i, i - GROUPS // 2)

    def work(i, c):
        g = place(i)

        @pl.when(i == GROUPS // 2)
        def _():
            group0 = out_blocks.at[pl.ds(0, GS)]
            pltpu.make_async_copy(group0, group0, d_send.at[0]).wait()
            lax.fori_loop(GS, Z // 2 - 1, send_out, 0)

        pltpu.make_async_copy(group(arrived, g), group(arrived, g), d_recv.at[g]).wait()
        forward(g).start()
        unpack(arrived, g, 0)

        @pl.when(i == GROUPS // 2)
        def _():
            finish(place(i - 1))
            send_group(place(i - 1))

        @pl.when((i > 0) & (i != GROUPS // 2))
        def _():
            finish(place(i - 1))

        @pl.when(i > GROUPS // 2)
        def _():
            send_group(place(i - 1))

        forward(g).wait_recv()
        unpack(sib_arrived, g, ROWS)
        total[...] = jnp.zeros_like(total)

        def hidden_chunk(i, c):
            cols = pl.ds(pl.multiple_of(i * FFC, FFC), FFC)
            hidden = jax.nn.gelu(dot(x_rows[...], win[:, cols])).astype(bf16)
            total[...] += dot(hidden, wout[cols, :])
            return c

        lax.fori_loop(0, win.shape[1] // FFC, hidden_chunk, 0)
        own_part[g] = total[0:ROWS].astype(bf16)
        send_part[g] = total[ROWS:2 * ROWS].astype(bf16)
        swap(g).start()
        return c

    lax.fori_loop(0, GROUPS, work, 0)
    finish(GROUPS // 2 - 1)

    send_group(GROUPS // 2 - 1)
    send_group(GROUPS - 1)

    def collect(g, c):
        pltpu.make_async_copy(group(ret_arrived, g), group(ret_arrived, g), r_recv.at[g]).wait()
        unpack(ret_arrived, g, 0)
        mask = (slot_col_ref[...] == g * ROWS + iota((tokens, ROWS), 1)).astype(bf16)
        token_total[...] += dot(mask, x_rows[0:ROWS])
        return c

    lax.fori_loop(0, GROUPS, collect, 0)

    layer_out = (tok[...].astype(f32) + gate_ref[...] * token_total[...]).astype(bf16)
    out_ref[...] = layer_out
    store = pltpu.make_async_copy(out_ref, out_hbm, w_sem.at[0])
    store.start()

    UR = 16
    row, at = iota((UR, tokens), 0), iota((UR, tokens), 1)
    first = jnp.where((row == 0) | (row == 2), 0, half)
    length = jnp.where(row == 2, clen[0], clen[1])
    start = jnp.where(row < 2, first, first + IMG_TOK)
    stop = first + IMG_TOK + jnp.where(row < 2, 0, length)
    pool = ((at >= start) & (at < stop) & (row < 4)).astype(bf16)
    row1 = iota((UR, 1), 0)
    count = jnp.where(row1 < 2, IMG_TOK, jnp.where(row1 == 2, clen[0], clen[1])).astype(f32)
    vectors = dot(pool, layer_out) / count
    squares = jnp.sum(vectors * vectors, axis=1, keepdims=True) + norm_eps
    unit = (vectors * lax.rsqrt(squares)).astype(bf16)
    gram = logit_scale * dot_nt(unit, unit)
    gram_row, gram_col = iota((UR, UR), 0), iota((UR, UR), 1)

    def pick(i):
        hit = (gram_row == i) & (gram_col == i + 2)
        return jnp.sum(jnp.sum(jnp.where(hit, gram, 0.0), axis=1, keepdims=True), axis=0, keepdims=True)

    stacked = jnp.concatenate([unit[:, j * LANES:(j + 1) * LANES] for j in range(CH)], axis=0)
    to = iota((2 * UR, 1), 0)
    inner = to % (2 * CH)
    source = (inner // 2) * UR + (to // (2 * CH)) * 2 + inner % 2
    select = (iota((2 * UR, CH * UR), 1) == source).astype(bf16)
    packed = dot(select, stacked).astype(bf16)
    units[0] = packed[0:UR]
    units[1] = packed[UR:2 * UR]

    def send_images(i, c):
        pltpu.make_async_remote_copy(
            src_ref=units.at[0], dst_ref=image_blocks.at[0, i], send_sem=g_send.at[0],
            recv_sem=g_recv.at[0], device_id=along_x(0, -image_offset(Z, i)), device_id_type=MESH,
        ).start()
        return c

    def send_texts(j, c):
        pltpu.make_async_remote_copy(
            src_ref=units.at[1], dst_ref=text_blocks.at[0, j], send_sem=g_send.at[1],
            recv_sem=g_recv.at[1], device_id=along_x(0, -caption_offset(Z, j)), device_id_type=MESH,
        ).start()
        return c

    own = 1 if NA == Z else 0
    lax.fori_loop(1, NB, send_texts, 0)
    lax.fori_loop(own, NA, send_images, 0)
    if own:
        image_blocks[0, 0] = packed[0:UR]
    text_blocks[0, 0] = packed[UR:2 * UR]
    row_vec[...] = jnp.zeros_like(row_vec)
    col_vec[...] = jnp.zeros_like(col_vec)

    def pass_images(m, c):
        pltpu.make_async_remote_copy(
            src_ref=image_blocks.at[0], dst_ref=image_blocks.at[m], send_sem=h_send.at[0],
            recv_sem=h_recv.at[0], device_id=along_x(m), device_id_type=MESH,
        ).start()
        return c

    def pass_texts(m, c):
        pltpu.make_async_remote_copy(
            src_ref=text_blocks.at[0], dst_ref=text_blocks.at[m], send_sem=h_send.at[1],
            recv_sem=h_recv.at[1], device_id=along_y(m), device_id_type=MESH,
        ).start()
        return c

    def all_of(part, sem):
        return pltpu.make_async_copy(part, part, sem)

    near_texts = text_blocks.at[0, pl.ds(min(1, NB - 1), max(1, NB - 1))]
    near_images = image_blocks.at[0, pl.ds(own, NA - own)]
    other_texts = text_blocks.at[pl.ds(1, YN * CORES - 1)]
    other_images = image_blocks.at[pl.ds(min(1, XN - 1), max(1, XN - 1))]
    if NB > 1:
        all_of(near_texts, g_recv.at[1]).wait()
    lax.fori_loop(1, YN * CORES, pass_texts, 0)
    all_of(near_images, g_recv.at[0]).wait()
    lax.fori_loop(1, XN, pass_images, 0)

    def lay_rows(blocks, matrix, rows_ref, n):
        rows = dot(matrix[...], blocks[...].reshape(n * UR, LANES)).astype(bf16)
        for j in range(CH):
            rows_ref[:, j * LANES:(j + 1) * LANES] = rows[j * 2 * n:(j + 1) * 2 * n]

    all_of(other_texts, h_recv.at[1]).wait()
    lay_rows(text_blocks, unfold_p, text_rows, NT)
    if XN > 1:
        all_of(other_images, h_recv.at[0]).wait()
    lay_rows(image_blocks, unfold_z, image_rows, NI)
    weights = once[...] * jnp.exp(logit_scale * dot_nt(image_rows[...], text_rows[...]))
    col_vec[:, 0:2 * NT] = jnp.sum(weights, axis=0, keepdims=True)
    eye_rows = iota((2 * NI, 2 * NI), 0) == iota((2 * NI, 2 * NI), 1)
    by_row = jnp.sum(weights, axis=1, keepdims=True)
    row_vec[:, 0:2 * NI] = jnp.sum(jnp.where(eye_rows, by_row, 0.0), axis=0, keepdims=True)

    def send_rows(n, c):
        pltpu.make_async_remote_copy(
            src_ref=row_vec, dst_ref=row_parts.at[n], send_sem=s_send.at[0], recv_sem=s_recv.at[0],
            device_id=along_x(XN - n // NA, image_offset(Z, n % NA)), device_id_type=MESH,
        ).start()
        return c

    def send_cols(n, c):
        m = n // NB
        back = (YN - m // CORES) * CORES + m % CORES
        pltpu.make_async_remote_copy(
            src_ref=col_vec, dst_ref=col_parts.at[n], send_sem=s_send.at[1], recv_sem=s_recv.at[1],
            device_id=along_y(back, caption_offset(Z, n % NB)), device_id_type=MESH,
        ).start()
        return c

    lax.fori_loop(1, NT, send_cols, 0)
    lax.fori_loop(own, NI, send_rows, 0)
    col_parts[0] = col_vec[...]
    if own:
        row_parts[0] = row_vec[...]

    def mine(parts, n, i):
        lane, at = iota((n, 1, LANES), 2), iota((n, 1, LANES), 0)
        kept = jnp.where(lane == 2 * at + i, parts, 0.0)
        return jnp.sum(jnp.sum(kept, axis=0), axis=1, keepdims=True)

    other_cols = col_parts.at[pl.ds(1, NT - 1)]
    other_rows = row_parts.at[pl.ds(own, NI - own)]
    all_of(other_cols, s_recv.at[1]).wait()
    col_total = [mine(col_parts[...], NT, i) for i in range(2)]
    all_of(other_rows, s_recv.at[0]).wait()
    row_total = [mine(row_parts[...], NI, i) for i in range(2)]
    losses = [
        0.5 * (jnp.log(row_total[i]) - pick(i)) + 0.5 * (jnp.log(col_total[i]) - pick(i))
        for i in range(2)
    ]
    loss_ref[...] = jnp.where(iota((1, LANES), 1) == 0, losses[0], losses[1])

    store.wait()
    def sent(part, sem):
        pltpu.make_async_copy(part, part, sem).wait()

    for g in range(1, GROUPS):
        count = GS - 1 if g == GROUPS - 1 else GS
        sent(out_blocks.at[pl.ds(g * GS, count)], d_send.at[g])
    sent(ret_blocks.at[pl.ds(0, Z - 1)], r_send)

    def drain(g, c):
        forward(g).wait_send()
        swap(g).wait_send()
        return c

    lax.fori_loop(0, GROUPS, drain, 0)
    all_of(near_images, g_send.at[0]).wait()
    if NB > 1:
        all_of(near_texts, g_send.at[1]).wait()
    if XN > 1:
        all_of(other_images, h_send.at[0]).wait()
    all_of(other_texts, h_send.at[1]).wait()
    all_of(other_rows, s_send.at[0]).wait()
    all_of(other_cols, s_send.at[1]).wait()


def per_device(tokens, expert_ids, caption_len, router, expert_in, expert_out, *, cfg):
    pairs, seq, width = tokens.shape
    count = pairs * seq
    Z, DP, CAP, CH, GS, FFC = cfg
    XN, YN = plane_shape(DP)
    NA, NB, _ = meeting(Z)
    NI, NT = XN * NA, YN * CORES * NB
    GROUPS = Z // GS
    BLK = CAP * CH
    ROWS = GS * CAP
    hidden = expert_in.shape[2]
    vmem = pl.BlockSpec(memory_space=pltpu.VMEM)
    hbm = pl.BlockSpec(memory_space=pltpu.HBM)
    dma = pltpu.SemaphoreType.DMA
    blocks = pltpu.VMEM((Z, BLK, LANES), bf16)
    parts = pltpu.VMEM((GROUPS, ROWS, width), bf16)
    out, loss = pl.pallas_call(
        functools.partial(kernel, cfg),
        out_shape=(
            jax.ShapeDtypeStruct((count, width), bf16),
            jax.ShapeDtypeStruct((1, LANES), f32),
        ),
        in_specs=[
            hbm, hbm, hbm, hbm, hbm, hbm,
        ],
        out_specs=(hbm, vmem),
        scratch_shapes=[
            pltpu.VMEM((count, width), bf16),
            pltpu.VMEM((pairs, 1, seq), jnp.int32),
            pltpu.SMEM((pairs,), jnp.int32),
            pltpu.VMEM((Z, width), bf16),
            pltpu.VMEM((count, width), bf16),
            pltpu.VMEM((width, hidden), bf16),
            pltpu.VMEM((hidden, width), bf16),
            pltpu.VMEM((GS * BLK, GS * BLK), bf16),
            pltpu.VMEM((GS * BLK, GS * BLK), bf16),
            pltpu.VMEM((NI * 16, NI * 16), bf16),
            pltpu.VMEM((NT * 16, NT * 16), bf16),
            pltpu.VMEM((count, 1), jnp.int32),
            pltpu.VMEM((count, 1), f32),
            blocks, blocks, blocks,
            pltpu.VMEM((2 * ROWS, width), bf16),
            pltpu.VMEM((2 * ROWS, width), f32),
            parts, parts, parts, blocks, blocks,
            pltpu.VMEM((count, width), f32),
            pltpu.VMEM((2, 16, LANES), bf16),
            pltpu.VMEM((XN, NA, 16, LANES), bf16),
            pltpu.VMEM((YN * CORES, NB, 16, LANES), bf16),
            pltpu.VMEM((2 * NI, width), bf16),
            pltpu.VMEM((2 * NT, width), bf16),
            pltpu.VMEM((2 * NI, 2 * NT), f32),
            pltpu.VMEM((1, LANES), f32),
            pltpu.VMEM((1, LANES), f32),
            pltpu.VMEM((NI, 1, LANES), f32),
            pltpu.VMEM((NT, 1, LANES), f32),
            dma((6,)), pltpu.SemaphoreType.REGULAR((2,)), dma((GROUPS,)), dma((GROUPS,)), dma((GROUPS,)), dma((GROUPS,)),
            dma((GROUPS,)), dma((GROUPS,)), dma, dma((GROUPS,)),
            dma((2,)), dma((2,)), dma((2,)), dma((2,)), dma((2,)), dma((2,)),
        ],
        compiler_params=pltpu.CompilerParams(
            collective_id=0, has_side_effects=True, vmem_limit_bytes=64 << 20
        ),
        cost_estimate=pl.CostEstimate(
            flops=8 * Z * CAP * width * hidden, bytes_accessed=4 * width * hidden, transcendentals=0
        ),
        name="expert_contrast",
    )(
        tokens.reshape(count, width),
        jnp.swapaxes(expert_ids, 1, 2),
        caption_len,
        router.T,
        expert_in,
        expert_out,
    )
    return out.reshape(pairs, seq, width), loss[0, :pairs]


def solution(mesh, cap=6, group=8, ff_chunk=512):
    cfg = (mesh.shape["expert"] // CORES, mesh.shape["dp"], cap, 8, group, ff_chunk)
    return jax.shard_map(
        functools.partial(per_device, cfg=cfg),
        mesh=mesh,
        in_specs=(
            P(("dp", "expert"), None, None),
            P(("dp", "expert"), None, None),
            P(("dp", "expert")),
            P(),
            P("expert", None, None),
            P("expert", None, None),
        ),
        out_specs=(P(("dp", "expert"), None, None), P(("dp", "expert"))),
        check_vma=False,
    )
```

```python
import functools

import jax
import jax.numpy as jnp
from jax import lax
from jax.experimental import pallas as pl
from jax.experimental.pallas import tpu as pltpu
from jax.sharding import PartitionSpec as P

IMG_TOK = 48
LANES = 128
CORES = 2
logit_scale = 20.0
norm_eps = 1e-06
MESH = pl.DeviceIdType.MESH
bf16 = jnp.bfloat16
f32 = jnp.float32


def iota(shape, axis):
    return lax.broadcasted_iota(jnp.int32, shape, axis)


def dot(a, b):
    return jnp.dot(a, b, preferred_element_type=f32)


def dot_nt(a, b):
    return lax.dot_general(a, b, (((1,), (1,)), ((), ())), preferred_element_type=f32)


def chunk_major(blocks, chunks, rows):
    size = blocks * chunks * rows
    to = iota((size, 1), 0)
    chunk, rest = to // (blocks * rows), to % (blocks * rows)
    source = (rest // rows) * (chunks * rows) + chunk * rows + rest % rows
    return (iota((size, size), 1) == source).astype(bf16)


def block_major(blocks, chunks, rows):
    size = blocks * chunks * rows
    to = iota((size, 1), 0)
    block, rest = to // (chunks * rows), to % (chunks * rows)
    source = (rest // rows) * (blocks * rows) + block * rows + rest % rows
    return (iota((size, size), 1) == source).astype(bf16)


def plane_shape(DP):
    XN = 1
    while 4 * XN * XN <= DP:
        XN *= 2
    return XN, DP // XN


def meeting(Z):
    if Z % 32:
        return Z, 1, []
    images, captions = 8, 5
    seen, repeated = set(), []
    for i in range(images):
        for j in range(captions):
            apart = (image_offset(Z, i) - caption_offset(Z, j)) % Z
            if apart in seen:
                repeated.append((i, j))
            seen.add(apart)
    assert len(seen) == Z
    return images, captions, repeated


def image_offset(Z, i):
    if Z % 32:
        return i
    return (Z // 4 - i // 2) * (1 - 2 * (i % 2))


def caption_offset(Z, j):
    if Z % 32:
        return 0 * j
    size = Z // 4 - (j - 1) // 2 * (Z // 8)
    return (1 - (j == 0)) * size * (1 - 2 * (j % 2))


def kernel(
    cfg, tok_hbm, ids_hbm, clen_hbm, router_hbm, win_hbm, wout_hbm, out_hbm, loss_hbm,
    tok, ids, clen, router_t, out_ref, loss_ref, win, wout, unfold, fold, unfold_z, unfold_p, slot_col_ref, gate_ref,
    out_blocks, arrived, sib_arrived, x_rows, total,
    own_part, send_part, sib_part, ret_blocks, ret_arrived, token_total,
    units, image_blocks, text_blocks, image_rows, text_rows, once,
    row_vec, col_vec, row_parts, col_parts,
    w_sem, far_sem, core_sem, d_send, d_recv, f_send, f_recv, p_send, p_recv, r_send, r_recv,
    g_send, g_recv, h_send, h_recv, s_send, s_recv,
):
    Z, DP, CAP, CH, GS, FFC = cfg
    XN, YN = plane_shape(DP)
    GROUPS = Z // GS
    BLK = CAP * CH
    ROWS = GS * CAP
    NA, NB, repeated = meeting(Z)
    NI, NT = XN * NA, YN * CORES * NB
    tokens = tok.shape[0]
    half = tokens // 2
    dp = lax.axis_index("dp")
    ex = lax.axis_index("expert")
    z = ex // CORES
    core = ex % CORES

    def ring(k):
        return {"dp": dp, "expert": lax.rem(z + k, Z) * CORES + core}

    x, y = dp // YN, dp % YN

    def along_x(dx, dz=0):
        return {
            "dp": lax.rem(x + dx, XN) * YN + y,
            "expert": lax.rem(z + dz + Z, Z) * CORES + core,
        }

    def along_y(m, dz=0):
        return {
            "dp": x * YN + lax.rem(y + m // CORES, YN),
            "expert": lax.rem(z + dz + Z, Z) * CORES + lax.rem(core + m % CORES, CORES),
        }

    sibling = {"dp": dp, "expert": z * CORES + (1 - core)}

    def offset(q):
        return jnp.where(q % 2 == 1, Z // 2 - (q + 1) // 2, lax.rem(q // 2 + Z // 2, Z))

    barrier = pltpu.get_barrier_semaphore()

    def greet_ring(k, c):
        pl.semaphore_signal(barrier, inc=1, device_id=ring(k), device_id_type=MESH)
        return c

    def greet_x(m, c):
        pl.semaphore_signal(barrier, inc=1, device_id=along_x(m), device_id_type=MESH)
        return c

    def greet_y(m, c):
        pl.semaphore_signal(barrier, inc=1, device_id=along_y(m * CORES), device_id_type=MESH)
        return c

    def greet_other_core(m, c):
        pl.semaphore_signal(barrier, inc=1, device_id=along_y(m * CORES + 1), device_id_type=MESH)
        return c

    def answer_other_core(m, c):
        pl.semaphore_signal(core_sem, inc=1, device_id=along_y(m * CORES + 1), device_id_type=MESH)
        return c

    NEAR = Z // 8
    load_ids = pltpu.make_async_copy(ids_hbm, ids, w_sem.at[0])
    load_tok = pltpu.make_async_copy(tok_hbm, tok, w_sem.at[1])
    load_router = pltpu.make_async_copy(router_hbm, router_t, w_sem.at[2])
    load_clen = pltpu.make_async_copy(clen_hbm, clen, w_sem.at[3])
    load_in = pltpu.make_async_copy(win_hbm.at[0], win, w_sem.at[4])
    load_out = pltpu.make_async_copy(wout_hbm.at[0], wout, w_sem.at[5])
    load_ids.start()
    load_tok.start()
    lax.fori_loop(1, NEAR + 1, greet_ring, 0)
    lax.fori_loop(Z - NEAR, Z, greet_ring, 0)
    lax.fori_loop(1, XN, greet_x, 0)
    lax.fori_loop(1, YN, greet_y, 0)
    lax.fori_loop(0, YN * (1 - core), greet_other_core, 0)
    load_router.start()
    load_clen.start()
    load_in.start()
    load_out.start()

    fold[...] = block_major(GS, CH, CAP)
    load_ids.wait()
    ids_row = jnp.concatenate([ids[0], ids[1]], axis=1)
    eye = iota((tokens, tokens), 0) == iota((tokens, tokens), 1)
    onehot_t = iota((Z, tokens), 0) == ids_row
    upto = (iota((tokens, tokens), 0) <= iota((tokens, tokens), 1)).astype(bf16)
    running = dot(onehot_t.astype(bf16), upto)
    position = jnp.sum(jnp.where(onehot_t, running, 0.0), axis=0, keepdims=True).astype(jnp.int32) - 1
    ahead = ids_row - z
    ahead = jnp.where(ahead < 0, ahead + Z, ahead)
    signed = jnp.where(ahead > Z // 2, ahead - Z, ahead)
    away = jnp.abs(signed)
    order = 2 * (Z // 2 - away) - jnp.where((signed >= 0) & (away < Z // 2), 1, 0)
    slot_row = order * CAP + position
    slot_col_ref[...] = jnp.sum(jnp.where(eye, slot_row.astype(f32), 0.0), axis=1, keepdims=True).astype(jnp.int32)
    ids_col = jnp.sum(jnp.where(eye, ids_row.astype(f32), 0.0), axis=1, keepdims=True).astype(jnp.int32)

    load_tok.wait()

    def pack(i, c):
        g = GROUPS - 1 - i
        mask = (slot_row == g * ROWS + iota((ROWS, tokens), 0)).astype(bf16)
        rows = dot(mask, tok[...]).astype(bf16)
        stacked = jnp.concatenate([rows[:, j * LANES:(j + 1) * LANES] for j in range(CH)], axis=0)
        out_blocks[pl.ds(g * GS, GS)] = dot(fold[...], stacked).astype(bf16).reshape(GS, BLK, LANES)
        return c

    lax.fori_loop(0, GROUPS, pack, 0)

    def send_out(q, c):
        pltpu.make_async_remote_copy(
            src_ref=out_blocks.at[q], dst_ref=arrived.at[q], send_sem=d_send.at[q // GS],
            recv_sem=d_recv.at[q // GS], device_id=ring(offset(q)), device_id_type=MESH,
        ).start()
        return c

    def tell(step, distance):
        for end in (distance, Z - distance):
            pl.semaphore_signal(far_sem.at[step], inc=1, device_id=ring(end), device_id_type=MESH)

    pl.semaphore_wait(barrier, 2 * NEAR + XN - 1 + YN - 1 + YN * core)
    tell(0, NEAR)
    lax.fori_loop(0, YN * core, answer_other_core, 0)
    lax.fori_loop(Z * 3 // 4 - 1, Z - 1, send_out, 0)
    pltpu.make_async_copy(out_blocks.at[Z - 1], arrived.at[Z - 1], d_recv.at[GROUPS - 1]).start()
    unfold[...] = chunk_major(GS, CH, CAP)
    pl.semaphore_wait(far_sem.at[0], 2)
    tell(1, 2 * NEAR)
    lax.fori_loop(Z // 2 - 1, Z * 3 // 4 - 1, send_out, 0)
    pl.semaphore_wait(far_sem.at[1], 2)
    lax.fori_loop(0, GS, send_out, 0)

    load_router.wait()
    load_clen.wait()
    logits = dot_nt(tok[...], router_t[...])
    onehot = iota((tokens, Z), 1) == ids_col
    gate_ref[...] = jax.nn.sigmoid(jnp.sum(jnp.where(onehot, logits, 0.0), axis=1, keepdims=True))
    token_total[...] = jnp.zeros_like(token_total)
    unfold_z[...] = chunk_major(NI, CH, 2)
    unfold_p[...] = chunk_major(NT, CH, 2)
    image_at, caption_at = iota((2 * NI, 2 * NT), 0) // 2 % NA, iota((2 * NI, 2 * NT), 1) // 2 % NB
    kept = jnp.ones((2 * NI, 2 * NT), f32)
    for i, j in repeated:
        kept = jnp.where((image_at == i) & (caption_at == j), 0.0, kept)
    once[...] = kept
    load_in.wait()
    load_out.wait()

    def group(ref, g):
        return ref.at[pl.ds(g * GS, GS)]

    def unpack(ref, g, base):
        blocks = ref[pl.ds(g * GS, GS)].reshape(GS * BLK, LANES)
        rows = dot(unfold[...], blocks).astype(bf16)
        for j in range(CH):
            x_rows[base:base + ROWS, j * LANES:(j + 1) * LANES] = rows[j * ROWS:(j + 1) * ROWS]

    def forward(g):
        return pltpu.make_async_remote_copy(
            src_ref=group(arrived, g), dst_ref=group(sib_arrived, g), send_sem=f_send.at[g],
            recv_sem=f_recv.at[g], device_id=sibling, device_id_type=MESH,
        )

    def swap(g):
        return pltpu.make_async_remote_copy(
            src_ref=send_part.at[g], dst_ref=sib_part.at[g], send_sem=p_send.at[g],
            recv_sem=p_recv.at[g], device_id=sibling, device_id_type=MESH,
        )

    def finish(g):
        swap(g).wait_recv()
        both = (own_part[g].astype(f32) + sib_part[g].astype(f32)).astype(bf16)
        stacked = jnp.concatenate([both[:, j * LANES:(j + 1) * LANES] for j in range(CH)], axis=0)
        ret_blocks[pl.ds(g * GS, GS)] = dot(fold[...], stacked).astype(bf16).reshape(GS, BLK, LANES)

    def send_group(g):
        def send_back(i, c):
            q = g * GS + i
            pltpu.make_async_remote_copy(
                src_ref=ret_blocks.at[q], dst_ref=ret_arrived.at[q], send_sem=r_send,
                recv_sem=r_recv.at[g], device_id=ring(Z - offset(q)), device_id_type=MESH,
            ).start()
            return c

        lax.fori_loop(0, jnp.where(g == GROUPS - 1, GS - 1, GS), send_back, 0)

        @pl.when(g == GROUPS - 1)
        def _():
            pltpu.make_async_copy(ret_blocks.at[Z - 1], ret_arrived.at[Z - 1], r_recv.at[g]).start()

    def place(i):
        return jnp.where(i < GROUPS // 2, GROUPS - 1 - i, i - GROUPS // 2)

    def work(i, c):
        g = place(i)

        @pl.when(i == GROUPS // 2)
        def _():
            group0 = out_blocks.at[pl.ds(0, GS)]
            pltpu.make_async_copy(group0, group0, d_send.at[0]).wait()
            lax.fori_loop(GS, Z // 2 - 1, send_out, 0)

        pltpu.make_async_copy(group(arrived, g), group(arrived, g), d_recv.at[g]).wait()
        forward(g).start()
        unpack(arrived, g, 0)

        @pl.when(i == GROUPS // 2)
        def _():
            finish(place(i - 1))
            send_group(place(i - 1))

        @pl.when((i > 0) & (i < GROUPS // 2))
        def _():
            finish(place(i - 1))

        forward(g).wait_recv()
        unpack(sib_arrived, g, ROWS)
        total[...] = jnp.zeros_like(total)

        def hidden_chunk(i, c):
            cols = pl.ds(pl.multiple_of(i * FFC, FFC), FFC)
            hidden = jax.nn.gelu(dot(x_rows[...], win[:, cols])).astype(bf16)
            total[...] += dot(hidden, wout[cols, :])
            return c

        lax.fori_loop(0, win.shape[1] // FFC, hidden_chunk, 0)
        own_part[g] = total[0:ROWS].astype(bf16)
        send_part[g] = total[ROWS:2 * ROWS].astype(bf16)
        swap(g).start()

        @pl.when(i >= GROUPS // 2)
        def _():
            finish(g)
            send_group(g)

        return c

    @pl.when(core == 0)
    def _():
        pl.semaphore_wait(core_sem, YN)

    lax.fori_loop(0, GROUPS, work, 0)
    send_group(GROUPS - 1)

    def collect(g, c):
        pltpu.make_async_copy(group(ret_arrived, g), group(ret_arrived, g), r_recv.at[g]).wait()
        unpack(ret_arrived, g, 0)
        mask = (slot_col_ref[...] == g * ROWS + iota((tokens, ROWS), 1)).astype(bf16)
        token_total[...] += dot(mask, x_rows[0:ROWS])
        return c

    lax.fori_loop(0, GROUPS, collect, 0)

    layer_out = (tok[...].astype(f32) + gate_ref[...] * token_total[...]).astype(bf16)
    out_ref[...] = layer_out
    store = pltpu.make_async_copy(out_ref, out_hbm, w_sem.at[0])
    store.start()

    UR = 16
    row, at = iota((UR, tokens), 0), iota((UR, tokens), 1)
    first = jnp.where((row == 0) | (row == 2), 0, half)
    length = jnp.where(row == 2, clen[0], clen[1])
    start = jnp.where(row < 2, first, first + IMG_TOK)
    stop = first + IMG_TOK + jnp.where(row < 2, 0, length)
    pool = ((at >= start) & (at < stop) & (row < 4)).astype(bf16)
    row1 = iota((UR, 1), 0)
    count = jnp.where(row1 < 2, IMG_TOK, jnp.where(row1 == 2, clen[0], clen[1])).astype(f32)
    vectors = dot(pool, layer_out) / count
    squares = jnp.sum(vectors * vectors, axis=1, keepdims=True) + norm_eps
    unit = (vectors * lax.rsqrt(squares)).astype(bf16)
    gram = logit_scale * dot_nt(unit, unit)
    gram_row, gram_col = iota((UR, UR), 0), iota((UR, UR), 1)

    def pick(i):
        hit = (gram_row == i) & (gram_col == i + 2)
        return jnp.sum(jnp.sum(jnp.where(hit, gram, 0.0), axis=1, keepdims=True), axis=0, keepdims=True)

    stacked = jnp.concatenate([unit[:, j * LANES:(j + 1) * LANES] for j in range(CH)], axis=0)
    to = iota((2 * UR, 1), 0)
    inner = to % (2 * CH)
    source = (inner // 2) * UR + (to // (2 * CH)) * 2 + inner % 2
    select = (iota((2 * UR, CH * UR), 1) == source).astype(bf16)
    packed = dot(select, stacked).astype(bf16)
    units[0] = packed[0:UR]
    units[1] = packed[UR:2 * UR]

    def send_images(i, c):
        pltpu.make_async_remote_copy(
            src_ref=units.at[0], dst_ref=image_blocks.at[0, i], send_sem=g_send.at[0],
            recv_sem=g_recv.at[0], device_id=along_x(0, -image_offset(Z, i)), device_id_type=MESH,
        ).start()
        return c

    def send_texts(j, c):
        pltpu.make_async_remote_copy(
            src_ref=units.at[1], dst_ref=text_blocks.at[0, j], send_sem=g_send.at[1],
            recv_sem=g_recv.at[1], device_id=along_x(0, -caption_offset(Z, j)), device_id_type=MESH,
        ).start()
        return c

    own = 1 if NA == Z else 0
    lax.fori_loop(1, NB, send_texts, 0)
    lax.fori_loop(own, NA, send_images, 0)
    if own:
        image_blocks[0, 0] = packed[0:UR]
    text_blocks[0, 0] = packed[UR:2 * UR]
    row_vec[...] = jnp.zeros_like(row_vec)
    col_vec[...] = jnp.zeros_like(col_vec)

    def pass_images(m, c):
        pltpu.make_async_remote_copy(
            src_ref=image_blocks.at[0], dst_ref=image_blocks.at[m], send_sem=h_send.at[0],
            recv_sem=h_recv.at[0], device_id=along_x(m), device_id_type=MESH,
        ).start()
        return c

    def pass_texts(m, c):
        pltpu.make_async_remote_copy(
            src_ref=text_blocks.at[0], dst_ref=text_blocks.at[m], send_sem=h_send.at[1],
            recv_sem=h_recv.at[1], device_id=along_y(m), device_id_type=MESH,
        ).start()
        return c

    def all_of(part, sem):
        return pltpu.make_async_copy(part, part, sem)

    near_texts = text_blocks.at[0, pl.ds(min(1, NB - 1), max(1, NB - 1))]
    near_images = image_blocks.at[0, pl.ds(own, NA - own)]
    other_texts = text_blocks.at[pl.ds(1, YN * CORES - 1)]
    other_images = image_blocks.at[pl.ds(min(1, XN - 1), max(1, XN - 1))]
    if NB > 1:
        all_of(near_texts, g_recv.at[1]).wait()
    lax.fori_loop(1, YN * CORES, pass_texts, 0)
    all_of(near_images, g_recv.at[0]).wait()
    lax.fori_loop(1, XN, pass_images, 0)

    def lay_rows(blocks, matrix, rows_ref, n):
        rows = dot(matrix[...], blocks[...].reshape(n * UR, LANES)).astype(bf16)
        for j in range(CH):
            rows_ref[:, j * LANES:(j + 1) * LANES] = rows[j * 2 * n:(j + 1) * 2 * n]

    all_of(other_texts, h_recv.at[1]).wait()
    lay_rows(text_blocks, unfold_p, text_rows, NT)
    if XN > 1:
        all_of(other_images, h_recv.at[0]).wait()
    lay_rows(image_blocks, unfold_z, image_rows, NI)
    weights = once[...] * jnp.exp(logit_scale * dot_nt(image_rows[...], text_rows[...]))
    col_vec[:, 0:2 * NT] = jnp.sum(weights, axis=0, keepdims=True)
    eye_rows = iota((2 * NI, 2 * NI), 0) == iota((2 * NI, 2 * NI), 1)
    by_row = jnp.sum(weights, axis=1, keepdims=True)
    row_vec[:, 0:2 * NI] = jnp.sum(jnp.where(eye_rows, by_row, 0.0), axis=0, keepdims=True)

    def send_rows(n, c):
        pltpu.make_async_remote_copy(
            src_ref=row_vec, dst_ref=row_parts.at[n], send_sem=s_send.at[0], recv_sem=s_recv.at[0],
            device_id=along_x(XN - n // NA, image_offset(Z, n % NA)), device_id_type=MESH,
        ).start()
        return c

    def send_cols(n, c):
        m = n // NB
        back = (YN - m // CORES) * CORES + m % CORES
        pltpu.make_async_remote_copy(
            src_ref=col_vec, dst_ref=col_parts.at[n], send_sem=s_send.at[1], recv_sem=s_recv.at[1],
            device_id=along_y(back, caption_offset(Z, n % NB)), device_id_type=MESH,
        ).start()
        return c

    lax.fori_loop(1, NT, send_cols, 0)
    lax.fori_loop(own, NI, send_rows, 0)
    col_parts[0] = col_vec[...]
    if own:
        row_parts[0] = row_vec[...]

    def mine(parts, n, i):
        lane, at = iota((n, 1, LANES), 2), iota((n, 1, LANES), 0)
        kept = jnp.where(lane == 2 * at + i, parts, 0.0)
        return jnp.sum(jnp.sum(kept, axis=0), axis=1, keepdims=True)

    other_cols = col_parts.at[pl.ds(1, NT - 1)]
    other_rows = row_parts.at[pl.ds(own, NI - own)]
    all_of(other_cols, s_recv.at[1]).wait()
    col_total = [mine(col_parts[...], NT, i) for i in range(2)]
    all_of(other_rows, s_recv.at[0]).wait()
    row_total = [mine(row_parts[...], NI, i) for i in range(2)]
    losses = [
        0.5 * (jnp.log(row_total[i]) - pick(i)) + 0.5 * (jnp.log(col_total[i]) - pick(i))
        for i in range(2)
    ]
    for i in range(2):
        loss_ref[i] = jnp.sum(losses[i])
    store_loss = pltpu.make_async_copy(loss_ref, loss_hbm, w_sem.at[1])
    store_loss.start()

    store.wait()
    store_loss.wait()
    def sent(part, sem):
        pltpu.make_async_copy(part, part, sem).wait()

    for g in range(1, GROUPS):
        count = GS - 1 if g == GROUPS - 1 else GS
        sent(out_blocks.at[pl.ds(g * GS, count)], d_send.at[g])
    sent(ret_blocks.at[pl.ds(0, Z - 1)], r_send)

    def drain(g, c):
        forward(g).wait_send()
        swap(g).wait_send()
        return c

    lax.fori_loop(0, GROUPS, drain, 0)
    all_of(near_images, g_send.at[0]).wait()
    if NB > 1:
        all_of(near_texts, g_send.at[1]).wait()
    if XN > 1:
        all_of(other_images, h_send.at[0]).wait()
    all_of(other_texts, h_send.at[1]).wait()
    all_of(other_rows, s_send.at[0]).wait()
    all_of(other_cols, s_send.at[1]).wait()


def hand_over(out, loss, out_result, loss_result):
    out_result[...] = out[...]
    loss_result[...] = loss[...]


def per_device(tokens, expert_ids, caption_len, router, expert_in, expert_out, *, cfg):
    pairs, seq, width = tokens.shape
    count = pairs * seq
    Z, DP, CAP, CH, GS, FFC = cfg
    XN, YN = plane_shape(DP)
    NA, NB, _ = meeting(Z)
    NI, NT = XN * NA, YN * CORES * NB
    GROUPS = Z // GS
    BLK = CAP * CH
    ROWS = GS * CAP
    hidden = expert_in.shape[2]
    hbm = pl.BlockSpec(memory_space=pltpu.HBM)
    dma = pltpu.SemaphoreType.DMA
    blocks = pltpu.VMEM((Z, BLK, LANES), bf16)
    parts = pltpu.VMEM((GROUPS, ROWS, width), bf16)
    out, loss = pl.pallas_call(
        functools.partial(kernel, cfg),
        out_shape=(
            jax.ShapeDtypeStruct((count, width), bf16),
            jax.ShapeDtypeStruct((pairs,), f32),
        ),
        in_specs=[
            hbm, hbm, hbm, hbm, hbm, hbm,
        ],
        out_specs=(hbm, hbm),
        scratch_shapes=[
            pltpu.VMEM((count, width), bf16),
            pltpu.VMEM((pairs, 1, seq), jnp.int32),
            pltpu.SMEM((pairs,), jnp.int32),
            pltpu.VMEM((Z, width), bf16),
            pltpu.VMEM((count, width), bf16),
            pltpu.SMEM((pairs,), f32),
            pltpu.VMEM((width, hidden), bf16),
            pltpu.VMEM((hidden, width), bf16),
            pltpu.VMEM((GS * BLK, GS * BLK), bf16),
            pltpu.VMEM((GS * BLK, GS * BLK), bf16),
            pltpu.VMEM((NI * 16, NI * 16), bf16),
            pltpu.VMEM((NT * 16, NT * 16), bf16),
            pltpu.VMEM((count, 1), jnp.int32),
            pltpu.VMEM((count, 1), f32),
            blocks, blocks, blocks,
            pltpu.VMEM((2 * ROWS, width), bf16),
            pltpu.VMEM((2 * ROWS, width), f32),
            parts, parts, parts, blocks, blocks,
            pltpu.VMEM((count, width), f32),
            pltpu.VMEM((2, 16, LANES), bf16),
            pltpu.VMEM((XN, NA, 16, LANES), bf16),
            pltpu.VMEM((YN * CORES, NB, 16, LANES), bf16),
            pltpu.VMEM((2 * NI, width), bf16),
            pltpu.VMEM((2 * NT, width), bf16),
            pltpu.VMEM((2 * NI, 2 * NT), f32),
            pltpu.VMEM((1, LANES), f32),
            pltpu.VMEM((1, LANES), f32),
            pltpu.VMEM((NI, 1, LANES), f32),
            pltpu.VMEM((NT, 1, LANES), f32),
            dma((6,)), pltpu.SemaphoreType.REGULAR((2,)), pltpu.SemaphoreType.REGULAR, dma((GROUPS,)), dma((GROUPS,)), dma((GROUPS,)), dma((GROUPS,)),
            dma((GROUPS,)), dma((GROUPS,)), dma, dma((GROUPS,)),
            dma((2,)), dma((2,)), dma((2,)), dma((2,)), dma((2,)), dma((2,)),
        ],
        compiler_params=pltpu.CompilerParams(
            collective_id=0, has_side_effects=True, vmem_limit_bytes=64 << 20
        ),
        cost_estimate=pl.CostEstimate(
            flops=8 * Z * CAP * width * hidden, bytes_accessed=4 * width * hidden, transcendentals=0
        ),
        name="expert_contrast",
    )(
        tokens.reshape(count, width),
        jnp.swapaxes(expert_ids, 1, 2),
        caption_len,
        router.T,
        expert_in,
        expert_out,
    )
    vmem = pl.BlockSpec(memory_space=pltpu.VMEM)
    out, loss = pl.pallas_call(
        hand_over,
        out_shape=(
            jax.ShapeDtypeStruct((count, width), bf16),
            jax.ShapeDtypeStruct((pairs,), f32),
        ),
        in_specs=[vmem, vmem],
        out_specs=(vmem, vmem),
        compiler_params=pltpu.CompilerParams(vmem_limit_bytes=64 << 20),
        name="hand_over",
    )(out, loss)
    return out.reshape(pairs, seq, width), loss


def solution(mesh, cap=6, group=8, ff_chunk=512):
    cfg = (mesh.shape["expert"] // CORES, mesh.shape["dp"], cap, 8, group, ff_chunk)
    return jax.shard_map(
        functools.partial(per_device, cfg=cfg),
        mesh=mesh,
        in_specs=(
            P(("dp", "expert"), None, None),
            P(("dp", "expert"), None, None),
            P(("dp", "expert")),
            P(),
            P("expert", None, None),
            P("expert", None, None),
        ),
        out_specs=(P(("dp", "expert"), None, None), P(("dp", "expert"))),
        check_vma=False,
    )
```

```python
import functools

import jax
import jax.numpy as jnp
from jax import lax
from jax.experimental import pallas as pl
from jax.experimental.pallas import tpu as pltpu
from jax.sharding import PartitionSpec as P

IMG_TOK = 48
LANES = 128
CORES = 2
logit_scale = 20.0
norm_eps = 1e-06
MESH = pl.DeviceIdType.MESH
bf16 = jnp.bfloat16
f32 = jnp.float32


def iota(shape, axis):
    return lax.broadcasted_iota(jnp.int32, shape, axis)


def dot(a, b):
    return jnp.dot(a, b, preferred_element_type=f32)


def dot_nt(a, b):
    return lax.dot_general(a, b, (((1,), (1,)), ((), ())), preferred_element_type=f32)


def chunk_major(blocks, chunks, rows):
    size = blocks * chunks * rows
    to = iota((size, 1), 0)
    chunk, rest = to // (blocks * rows), to % (blocks * rows)
    source = (rest // rows) * (chunks * rows) + chunk * rows + rest % rows
    return (iota((size, size), 1) == source).astype(bf16)


def block_major(blocks, chunks, rows):
    size = blocks * chunks * rows
    to = iota((size, 1), 0)
    block, rest = to // (chunks * rows), to % (chunks * rows)
    source = (rest // rows) * (blocks * rows) + block * rows + rest % rows
    return (iota((size, size), 1) == source).astype(bf16)


def plane_shape(DP):
    XN = 1
    while 4 * XN * XN <= DP:
        XN *= 2
    return XN, DP // XN


def meeting(Z):
    if Z % 32:
        return Z, 1, []
    images, captions = 8, 5
    seen, repeated = set(), []
    for i in range(images):
        for j in range(captions):
            apart = (image_offset(Z, i) - caption_offset(Z, j)) % Z
            if apart in seen:
                repeated.append((i, j))
            seen.add(apart)
    assert len(seen) == Z
    return images, captions, repeated


def image_offset(Z, i):
    if Z % 32:
        return i
    return (Z // 4 - i // 2) * (1 - 2 * (i % 2))


def caption_offset(Z, j):
    if Z % 32:
        return 0 * j
    size = Z // 4 - (j - 1) // 2 * (Z // 8)
    return (1 - (j == 0)) * size * (1 - 2 * (j % 2))


def kernel(
    cfg, tok_hbm, ids_hbm, clen_hbm, router_hbm, win_hbm, wout_hbm, out_hbm, loss_hbm,
    tok, ids, clen, router_t, out_ref, loss_ref, win, wout, unfold, fold, unfold_z, unfold_p, slot_col_ref, gate_ref,
    out_blocks, arrived, sib_arrived, x_rows, total,
    own_part, send_part, sib_part, ret_blocks, ret_arrived, token_total,
    units, image_blocks, text_blocks, image_rows, text_rows, once,
    row_vec, col_vec, row_parts, col_parts,
    w_sem, far_sem, core_sem, d_send, d_recv, f_send, f_recv, p_send, p_recv, r_send, r_recv,
    g_send, g_recv, h_send, h_recv, s_send, s_recv,
):
    Z, DP, CAP, CH, GS, FFC = cfg
    XN, YN = plane_shape(DP)
    GROUPS = Z // GS
    BLK = CAP * CH
    ROWS = GS * CAP
    NA, NB, repeated = meeting(Z)
    NI, NT = XN * NA, YN * CORES * NB
    tokens = tok.shape[0]
    half = tokens // 2
    dp = lax.axis_index("dp")
    ex = lax.axis_index("expert")
    z = ex // CORES
    core = ex % CORES

    def ring(k):
        return {"dp": dp, "expert": lax.rem(z + k, Z) * CORES + core}

    x, y = dp // YN, dp % YN

    def along_x(dx, dz=0):
        return {
            "dp": lax.rem(x + dx, XN) * YN + y,
            "expert": lax.rem(z + dz + Z, Z) * CORES + core,
        }

    def along_y(m, dz=0):
        return {
            "dp": x * YN + lax.rem(y + m // CORES, YN),
            "expert": lax.rem(z + dz + Z, Z) * CORES + lax.rem(core + m % CORES, CORES),
        }

    sibling = {"dp": dp, "expert": z * CORES + (1 - core)}

    def offset(q):
        up = jnp.where(q % 2 == 1, Z // 2 - (q + 1) // 2, lax.rem(q // 2 + Z // 2, Z))
        return lax.rem(Z + up * (1 - 2 * core), Z)

    barrier = pltpu.get_barrier_semaphore()

    def greet_ring(k, c):
        pl.semaphore_signal(barrier, inc=1, device_id=ring(k), device_id_type=MESH)
        return c

    def greet_x(m, c):
        pl.semaphore_signal(barrier, inc=1, device_id=along_x(m), device_id_type=MESH)
        return c

    def greet_y(m, c):
        pl.semaphore_signal(barrier, inc=1, device_id=along_y(m * CORES), device_id_type=MESH)
        return c

    def greet_other_core(m, c):
        pl.semaphore_signal(barrier, inc=1, device_id=along_y(m * CORES + 1), device_id_type=MESH)
        return c

    def answer_other_core(m, c):
        pl.semaphore_signal(core_sem, inc=1, device_id=along_y(m * CORES + 1), device_id_type=MESH)
        return c

    NEAR = Z // 8
    load_ids = pltpu.make_async_copy(ids_hbm, ids, w_sem.at[0])
    load_tok = pltpu.make_async_copy(tok_hbm, tok, w_sem.at[1])
    load_router = pltpu.make_async_copy(router_hbm, router_t, w_sem.at[2])
    load_clen = pltpu.make_async_copy(clen_hbm, clen, w_sem.at[3])
    load_in = pltpu.make_async_copy(win_hbm.at[0], win, w_sem.at[4])
    load_out = pltpu.make_async_copy(wout_hbm.at[0], wout, w_sem.at[5])
    load_ids.start()
    load_tok.start()
    lax.fori_loop(1, NEAR + 1, greet_ring, 0)
    lax.fori_loop(Z - NEAR, Z, greet_ring, 0)
    lax.fori_loop(1, XN, greet_x, 0)
    lax.fori_loop(1, YN, greet_y, 0)
    lax.fori_loop(0, YN * (1 - core), greet_other_core, 0)
    load_router.start()
    load_clen.start()
    load_in.start()
    load_out.start()

    fold[...] = block_major(GS, CH, CAP)
    load_ids.wait()
    ids_row = jnp.concatenate([ids[0], ids[1]], axis=1)
    eye = iota((tokens, tokens), 0) == iota((tokens, tokens), 1)
    onehot_t = iota((Z, tokens), 0) == ids_row
    upto = (iota((tokens, tokens), 0) <= iota((tokens, tokens), 1)).astype(bf16)
    running = dot(onehot_t.astype(bf16), upto)
    position = jnp.sum(jnp.where(onehot_t, running, 0.0), axis=0, keepdims=True).astype(jnp.int32) - 1
    ahead = (ids_row - z) * (1 - 2 * core)
    ahead = jnp.where(ahead < 0, ahead + Z, ahead)
    signed = jnp.where(ahead > Z // 2, ahead - Z, ahead)
    away = jnp.abs(signed)
    order = 2 * (Z // 2 - away) - jnp.where((signed >= 0) & (away < Z // 2), 1, 0)
    slot_row = order * CAP + position
    slot_col_ref[...] = jnp.sum(jnp.where(eye, slot_row.astype(f32), 0.0), axis=1, keepdims=True).astype(jnp.int32)
    ids_col = jnp.sum(jnp.where(eye, ids_row.astype(f32), 0.0), axis=1, keepdims=True).astype(jnp.int32)

    load_tok.wait()

    def pack(i, c):
        g = GROUPS - 1 - i
        mask = (slot_row == g * ROWS + iota((ROWS, tokens), 0)).astype(bf16)
        rows = dot(mask, tok[...]).astype(bf16)
        stacked = jnp.concatenate([rows[:, j * LANES:(j + 1) * LANES] for j in range(CH)], axis=0)
        out_blocks[pl.ds(g * GS, GS)] = dot(fold[...], stacked).astype(bf16).reshape(GS, BLK, LANES)
        return c

    lax.fori_loop(0, GROUPS // 2, pack, 0)

    def send_out(q, c):
        pltpu.make_async_remote_copy(
            src_ref=out_blocks.at[q], dst_ref=arrived.at[q], send_sem=d_send.at[q // GS],
            recv_sem=d_recv.at[q // GS], device_id=ring(offset(q)), device_id_type=MESH,
        ).start()
        return c

    def tell(step, distance):
        for end in (distance, Z - distance):
            pl.semaphore_signal(far_sem.at[step], inc=1, device_id=ring(end), device_id_type=MESH)

    pl.semaphore_wait(barrier, 2 * NEAR + XN - 1 + YN - 1 + YN * core)
    tell(0, NEAR)
    lax.fori_loop(0, YN * core, answer_other_core, 0)
    lax.fori_loop(Z * 3 // 4 - 1, Z - 1, send_out, 0)
    pltpu.make_async_copy(out_blocks.at[Z - 1], arrived.at[Z - 1], d_recv.at[GROUPS - 1]).start()
    lax.fori_loop(GROUPS // 2, GROUPS, pack, 0)
    pl.semaphore_wait(far_sem.at[0], 2)
    tell(1, 2 * NEAR)
    lax.fori_loop(Z // 2 - 1, Z * 3 // 4 - 1, send_out, 0)
    unfold[...] = chunk_major(GS, CH, CAP)
    pl.semaphore_wait(far_sem.at[1], 2)
    lax.fori_loop(0, GS, send_out, 0)

    load_router.wait()
    load_clen.wait()
    logits = dot_nt(tok[...], router_t[...])
    onehot = iota((tokens, Z), 1) == ids_col
    gate_ref[...] = jax.nn.sigmoid(jnp.sum(jnp.where(onehot, logits, 0.0), axis=1, keepdims=True))
    token_total[...] = jnp.zeros_like(token_total)
    unfold_z[...] = chunk_major(NI, CH, 2)
    unfold_p[...] = chunk_major(NT, CH, 2)
    image_at, caption_at = iota((2 * NI, 2 * NT), 0) // 2 % NA, iota((2 * NI, 2 * NT), 1) // 2 % NB
    kept = jnp.ones((2 * NI, 2 * NT), f32)
    for i, j in repeated:
        kept = jnp.where((image_at == i) & (caption_at == j), 0.0, kept)
    once[...] = kept
    load_in.wait()
    load_out.wait()

    def group(ref, g):
        return ref.at[pl.ds(g * GS, GS)]

    def unpack(ref, g, base):
        blocks = ref[pl.ds(g * GS, GS)].reshape(GS * BLK, LANES)
        rows = dot(unfold[...], blocks).astype(bf16)
        for j in range(CH):
            x_rows[base:base + ROWS, j * LANES:(j + 1) * LANES] = rows[j * ROWS:(j + 1) * ROWS]

    def forward(g):
        return pltpu.make_async_remote_copy(
            src_ref=group(arrived, g), dst_ref=group(sib_arrived, g), send_sem=f_send.at[g],
            recv_sem=f_recv.at[g], device_id=sibling, device_id_type=MESH,
        )

    def swap(g):
        return pltpu.make_async_remote_copy(
            src_ref=send_part.at[g], dst_ref=sib_part.at[g], send_sem=p_send.at[g],
            recv_sem=p_recv.at[g], device_id=sibling, device_id_type=MESH,
        )

    def finish(g):
        swap(g).wait_recv()
        both = (own_part[g].astype(f32) + sib_part[g].astype(f32)).astype(bf16)
        stacked = jnp.concatenate([both[:, j * LANES:(j + 1) * LANES] for j in range(CH)], axis=0)
        ret_blocks[pl.ds(g * GS, GS)] = dot(fold[...], stacked).astype(bf16).reshape(GS, BLK, LANES)

    def send_group(g):
        def send_back(i, c):
            q = g * GS + i
            pltpu.make_async_remote_copy(
                src_ref=ret_blocks.at[q], dst_ref=ret_arrived.at[q], send_sem=r_send,
                recv_sem=r_recv.at[g], device_id=ring(Z - offset(q)), device_id_type=MESH,
            ).start()
            return c

        lax.fori_loop(0, jnp.where(g == GROUPS - 1, GS - 1, GS), send_back, 0)

        @pl.when(g == GROUPS - 1)
        def _():
            pltpu.make_async_copy(ret_blocks.at[Z - 1], ret_arrived.at[Z - 1], r_recv.at[g]).start()

    def place(i):
        return jnp.where(i < GROUPS // 2, GROUPS - 1 - i, i - GROUPS // 2)

    def work(i, c):
        g = place(i)

        @pl.when(i == GROUPS // 2)
        def _():
            group0 = out_blocks.at[pl.ds(0, GS)]
            pltpu.make_async_copy(group0, group0, d_send.at[0]).wait()
            lax.fori_loop(GS, Z // 2 - 1, send_out, 0)

        pltpu.make_async_copy(group(arrived, g), group(arrived, g), d_recv.at[g]).wait()
        forward(g).start()
        unpack(arrived, g, 0)

        @pl.when(i == GROUPS // 2)
        def _():
            finish(place(i - 1))
            send_group(place(i - 1))

        @pl.when((i > 0) & (i < GROUPS // 2))
        def _():
            finish(place(i - 1))

        forward(g).wait_recv()
        unpack(sib_arrived, g, ROWS)
        total[...] = jnp.zeros_like(total)

        def hidden_chunk(i, c):
            cols = pl.ds(pl.multiple_of(i * FFC, FFC), FFC)
            hidden = jax.nn.gelu(dot(x_rows[...], win[:, cols])).astype(bf16)
            total[...] += dot(hidden, wout[cols, :])
            return c

        lax.fori_loop(0, win.shape[1] // FFC, hidden_chunk, 0)
        own_part[g] = total[0:ROWS].astype(bf16)
        send_part[g] = total[ROWS:2 * ROWS].astype(bf16)
        swap(g).start()

        @pl.when(i >= GROUPS // 2)
        def _():
            finish(g)
            send_group(g)

        return c

    @pl.when(core == 0)
    def _():
        pl.semaphore_wait(core_sem, YN)

    lax.fori_loop(0, GROUPS, work, 0)
    send_group(GROUPS - 1)

    def collect(g, c):
        pltpu.make_async_copy(group(ret_arrived, g), group(ret_arrived, g), r_recv.at[g]).wait()
        unpack(ret_arrived, g, 0)
        mask = (slot_col_ref[...] == g * ROWS + iota((tokens, ROWS), 1)).astype(bf16)
        token_total[...] += dot(mask, x_rows[0:ROWS])
        return c

    lax.fori_loop(0, GROUPS, collect, 0)

    layer_out = (tok[...].astype(f32) + gate_ref[...] * token_total[...]).astype(bf16)
    out_ref[...] = layer_out
    store = pltpu.make_async_copy(out_ref, out_hbm, w_sem.at[0])
    store.start()

    UR = 16
    row, at = iota((UR, tokens), 0), iota((UR, tokens), 1)
    first = jnp.where((row == 0) | (row == 2), 0, half)
    length = jnp.where(row == 2, clen[0], clen[1])
    start = jnp.where(row < 2, first, first + IMG_TOK)
    stop = first + IMG_TOK + jnp.where(row < 2, 0, length)
    pool = ((at >= start) & (at < stop) & (row < 4)).astype(bf16)
    row1 = iota((UR, 1), 0)
    count = jnp.where(row1 < 2, IMG_TOK, jnp.where(row1 == 2, clen[0], clen[1])).astype(f32)
    vectors = dot(pool, layer_out) / count
    squares = jnp.sum(vectors * vectors, axis=1, keepdims=True) + norm_eps
    unit = (vectors * lax.rsqrt(squares)).astype(bf16)
    gram = logit_scale * dot_nt(unit, unit)
    gram_row, gram_col = iota((UR, UR), 0), iota((UR, UR), 1)

    def pick(i):
        hit = (gram_row == i) & (gram_col == i + 2)
        return jnp.sum(jnp.sum(jnp.where(hit, gram, 0.0), axis=1, keepdims=True), axis=0, keepdims=True)

    stacked = jnp.concatenate([unit[:, j * LANES:(j + 1) * LANES] for j in range(CH)], axis=0)
    to = iota((2 * UR, 1), 0)
    inner = to % (2 * CH)
    source = (inner // 2) * UR + (to // (2 * CH)) * 2 + inner % 2
    select = (iota((2 * UR, CH * UR), 1) == source).astype(bf16)
    packed = dot(select, stacked).astype(bf16)
    units[0] = packed[0:UR]
    units[1] = packed[UR:2 * UR]

    def send_images(i, c):
        pltpu.make_async_remote_copy(
            src_ref=units.at[0], dst_ref=image_blocks.at[0, i], send_sem=g_send.at[0],
            recv_sem=g_recv.at[0], device_id=along_x(0, -image_offset(Z, i)), device_id_type=MESH,
        ).start()
        return c

    def send_texts(j, c):
        pltpu.make_async_remote_copy(
            src_ref=units.at[1], dst_ref=text_blocks.at[0, j], send_sem=g_send.at[1],
            recv_sem=g_recv.at[1], device_id=along_x(0, -caption_offset(Z, j)), device_id_type=MESH,
        ).start()
        return c

    own = 1 if NA == Z else 0
    lax.fori_loop(1, NB, send_texts, 0)
    lax.fori_loop(own, NA, send_images, 0)
    if own:
        image_blocks[0, 0] = packed[0:UR]
    text_blocks[0, 0] = packed[UR:2 * UR]
    row_vec[...] = jnp.zeros_like(row_vec)
    col_vec[...] = jnp.zeros_like(col_vec)

    def pass_images(m, c):
        pltpu.make_async_remote_copy(
            src_ref=image_blocks.at[0], dst_ref=image_blocks.at[m], send_sem=h_send.at[0],
            recv_sem=h_recv.at[0], device_id=along_x(m), device_id_type=MESH,
        ).start()
        return c

    def pass_texts(i, c):
        m = lax.rem(i + YN, YN * CORES)
        pltpu.make_async_remote_copy(
            src_ref=text_blocks.at[0], dst_ref=text_blocks.at[m], send_sem=h_send.at[1],
            recv_sem=h_recv.at[1], device_id=along_y(m), device_id_type=MESH,
        ).start()
        return c

    def all_of(part, sem):
        return pltpu.make_async_copy(part, part, sem)

    near_texts = text_blocks.at[0, pl.ds(min(1, NB - 1), max(1, NB - 1))]
    near_images = image_blocks.at[0, pl.ds(own, NA - own)]
    other_texts = text_blocks.at[pl.ds(1, YN * CORES - 1)]
    other_images = image_blocks.at[pl.ds(min(1, XN - 1), max(1, XN - 1))]
    if NB > 1:
        all_of(near_texts, g_recv.at[1]).wait()
    lax.fori_loop(0, YN, pass_texts, 0)
    lax.fori_loop(YN + 1, YN * CORES, pass_texts, 0)
    all_of(near_images, g_recv.at[0]).wait()
    lax.fori_loop(1, XN, pass_images, 0)

    def lay_rows(blocks, matrix, rows_ref, n):
        rows = dot(matrix[...], blocks[...].reshape(n * UR, LANES)).astype(bf16)
        for j in range(CH):
            rows_ref[:, j * LANES:(j + 1) * LANES] = rows[j * 2 * n:(j + 1) * 2 * n]

    all_of(other_texts, h_recv.at[1]).wait()
    lay_rows(text_blocks, unfold_p, text_rows, NT)
    if XN > 1:
        all_of(other_images, h_recv.at[0]).wait()
    lay_rows(image_blocks, unfold_z, image_rows, NI)
    weights = once[...] * jnp.exp(logit_scale * dot_nt(image_rows[...], text_rows[...]))
    col_vec[:, 0:2 * NT] = jnp.sum(weights, axis=0, keepdims=True)
    eye_rows = iota((2 * NI, 2 * NI), 0) == iota((2 * NI, 2 * NI), 1)
    by_row = jnp.sum(weights, axis=1, keepdims=True)
    row_vec[:, 0:2 * NI] = jnp.sum(jnp.where(eye_rows, by_row, 0.0), axis=0, keepdims=True)

    def send_rows(i, c):
        block, m = i // XN, lax.rem(i + XN // 2, XN)
        pltpu.make_async_remote_copy(
            src_ref=row_vec, dst_ref=row_parts.at[m * NA + block], send_sem=s_send.at[0], recv_sem=s_recv.at[0],
            device_id=along_x(XN - m, image_offset(Z, block)), device_id_type=MESH,
        ).start()
        return c

    def send_cols(i, c):
        block, m = lax.rem(i // (YN * CORES) + 1, NB), lax.rem(i + YN, YN * CORES)
        back = (YN - m // CORES) * CORES + m % CORES
        pltpu.make_async_remote_copy(
            src_ref=col_vec, dst_ref=col_parts.at[m * NB + block], send_sem=s_send.at[1], recv_sem=s_recv.at[1],
            device_id=along_y(back, caption_offset(Z, block)), device_id_type=MESH,
        ).start()
        return c

    own_col = (NB - 1) * YN * CORES + YN
    lax.fori_loop(0, own_col, send_cols, 0)
    lax.fori_loop(own_col + 1, NT, send_cols, 0)
    own_row = (XN - XN // 2) % XN if own else NI
    lax.fori_loop(0, own_row, send_rows, 0)
    lax.fori_loop(own_row + 1, NI, send_rows, 0)
    col_parts[0] = col_vec[...]
    if own:
        row_parts[0] = row_vec[...]

    def mine(parts, n, i):
        lane, at = iota((n, 1, LANES), 2), iota((n, 1, LANES), 0)
        kept = jnp.where(lane == 2 * at + i, parts, 0.0)
        return jnp.sum(jnp.sum(kept, axis=0), axis=1, keepdims=True)

    other_cols = col_parts.at[pl.ds(1, NT - 1)]
    other_rows = row_parts.at[pl.ds(own, NI - own)]
    all_of(other_cols, s_recv.at[1]).wait()
    col_total = [mine(col_parts[...], NT, i) for i in range(2)]
    all_of(other_rows, s_recv.at[0]).wait()
    row_total = [mine(row_parts[...], NI, i) for i in range(2)]
    losses = [
        0.5 * (jnp.log(row_total[i]) - pick(i)) + 0.5 * (jnp.log(col_total[i]) - pick(i))
        for i in range(2)
    ]
    for i in range(2):
        loss_ref[i] = jnp.sum(losses[i])
    store_loss = pltpu.make_async_copy(loss_ref, loss_hbm, w_sem.at[1])
    store_loss.start()

    store.wait()
    store_loss.wait()
    def sent(part, sem):
        pltpu.make_async_copy(part, part, sem).wait()

    for g in range(1, GROUPS):
        count = GS - 1 if g == GROUPS - 1 else GS
        sent(out_blocks.at[pl.ds(g * GS, count)], d_send.at[g])
    sent(ret_blocks.at[pl.ds(0, Z - 1)], r_send)

    def drain(g, c):
        forward(g).wait_send()
        swap(g).wait_send()
        return c

    lax.fori_loop(0, GROUPS, drain, 0)
    all_of(near_images, g_send.at[0]).wait()
    if NB > 1:
        all_of(near_texts, g_send.at[1]).wait()
    if XN > 1:
        all_of(other_images, h_send.at[0]).wait()
    all_of(other_texts, h_send.at[1]).wait()
    all_of(other_rows, s_send.at[0]).wait()
    all_of(other_cols, s_send.at[1]).wait()


def hand_over(out, loss, out_result, loss_result):
    out_result[...] = out[...]
    loss_result[...] = loss[...]


def per_device(tokens, expert_ids, caption_len, router, expert_in, expert_out, *, cfg):
    pairs, seq, width = tokens.shape
    count = pairs * seq
    Z, DP, CAP, CH, GS, FFC = cfg
    XN, YN = plane_shape(DP)
    NA, NB, _ = meeting(Z)
    NI, NT = XN * NA, YN * CORES * NB
    GROUPS = Z // GS
    BLK = CAP * CH
    ROWS = GS * CAP
    hidden = expert_in.shape[2]
    hbm = pl.BlockSpec(memory_space=pltpu.HBM)
    dma = pltpu.SemaphoreType.DMA
    blocks = pltpu.VMEM((Z, BLK, LANES), bf16)
    parts = pltpu.VMEM((GROUPS, ROWS, width), bf16)
    out, loss = pl.pallas_call(
        functools.partial(kernel, cfg),
        out_shape=(
            jax.ShapeDtypeStruct((count, width), bf16),
            jax.ShapeDtypeStruct((pairs,), f32),
        ),
        in_specs=[
            hbm, hbm, hbm, hbm, hbm, hbm,
        ],
        out_specs=(hbm, hbm),
        scratch_shapes=[
            pltpu.VMEM((count, width), bf16),
            pltpu.VMEM((pairs, 1, seq), jnp.int32),
            pltpu.SMEM((pairs,), jnp.int32),
            pltpu.VMEM((Z, width), bf16),
            pltpu.VMEM((count, width), bf16),
            pltpu.SMEM((pairs,), f32),
            pltpu.VMEM((width, hidden), bf16),
            pltpu.VMEM((hidden, width), bf16),
            pltpu.VMEM((GS * BLK, GS * BLK), bf16),
            pltpu.VMEM((GS * BLK, GS * BLK), bf16),
            pltpu.VMEM((NI * 16, NI * 16), bf16),
            pltpu.VMEM((NT * 16, NT * 16), bf16),
            pltpu.VMEM((count, 1), jnp.int32),
            pltpu.VMEM((count, 1), f32),
            blocks, blocks, blocks,
            pltpu.VMEM((2 * ROWS, width), bf16),
            pltpu.VMEM((2 * ROWS, width), f32),
            parts, parts, parts, blocks, blocks,
            pltpu.VMEM((count, width), f32),
            pltpu.VMEM((2, 16, LANES), bf16),
            pltpu.VMEM((XN, NA, 16, LANES), bf16),
            pltpu.VMEM((YN * CORES, NB, 16, LANES), bf16),
            pltpu.VMEM((2 * NI, width), bf16),
            pltpu.VMEM((2 * NT, width), bf16),
            pltpu.VMEM((2 * NI, 2 * NT), f32),
            pltpu.VMEM((1, LANES), f32),
            pltpu.VMEM((1, LANES), f32),
            pltpu.VMEM((NI, 1, LANES), f32),
            pltpu.VMEM((NT, 1, LANES), f32),
            dma((6,)), pltpu.SemaphoreType.REGULAR((2,)), pltpu.SemaphoreType.REGULAR, dma((GROUPS,)), dma((GROUPS,)), dma((GROUPS,)), dma((GROUPS,)),
            dma((GROUPS,)), dma((GROUPS,)), dma, dma((GROUPS,)),
            dma((2,)), dma((2,)), dma((2,)), dma((2,)), dma((2,)), dma((2,)),
        ],
        compiler_params=pltpu.CompilerParams(
            collective_id=0, has_side_effects=True, vmem_limit_bytes=64 << 20
        ),
        cost_estimate=pl.CostEstimate(
            flops=8 * Z * CAP * width * hidden, bytes_accessed=4 * width * hidden, transcendentals=0
        ),
        name="expert_contrast",
    )(
        tokens.reshape(count, width),
        jnp.swapaxes(expert_ids, 1, 2),
        caption_len,
        router.T,
        expert_in,
        expert_out,
    )
    vmem = pl.BlockSpec(memory_space=pltpu.VMEM)
    out, loss = pl.pallas_call(
        hand_over,
        out_shape=(
            jax.ShapeDtypeStruct((count, width), bf16),
            jax.ShapeDtypeStruct((pairs,), f32),
        ),
        in_specs=[vmem, vmem],
        out_specs=(vmem, vmem),
        compiler_params=pltpu.CompilerParams(vmem_limit_bytes=64 << 20),
        name="hand_over",
    )(out, loss)
    return out.reshape(pairs, seq, width), loss


def solution(mesh, cap=6, group=8, ff_chunk=512):
    cfg = (mesh.shape["expert"] // CORES, mesh.shape["dp"], cap, 8, group, ff_chunk)
    return jax.shard_map(
        functools.partial(per_device, cfg=cfg),
        mesh=mesh,
        in_specs=(
            P(("dp", "expert"), None, None),
            P(("dp", "expert"), None, None),
            P(("dp", "expert")),
            P(),
            P("expert", None, None),
            P("expert", None, None),
        ),
        out_specs=(P(("dp", "expert"), None, None), P(("dp", "expert"))),
        check_vma=False,
    )
```
